128 devices in a mesh: tile: 16 (over x, z_hi, core), plane: 8 (over z_lo, y).
Axes of the slice: x: 4, y: 4, z: 4 (z_hi: 2, z_lo: 2; z = z_hi * 2 + z_lo), core: 2. Of those that a mesh axis runs over, the one named last changes fastest.
Arguments:
- fields: float32 [2, 8, 128, 256, 256], P(None, 'plane', 'tile'), may hold values from -5 to 5
- amplitudes: float32 [8, 128, 256, 256], P('plane', 'tile'), may hold values from 0.3 to 3
- pupil: float32 [2, 256, 256], replicated, may hold values from -4 to 4
- distances: float32 [8], P('plane'), may hold values from 5 to 40
Outputs:
- new_fields: float32 [2, 8, 128, 256, 256], P(None, 'plane', 'tile')
- pupil_gradient: float32 [2, 256, 256], replicated
The draws below stay inside these ranges and needn't reach their ends.
All inputs are finite; a program needn't handle non-finite values.
Results may differ from the reference program's by a relative error of at most 0.0003.
Values sent between devices are 32-bit elements; how exact they have to be, the bound alone decides.
No kernel may reach another device: no remote copies, remote signals or barrier semaphores. Data moves between devices by JAX's collectives and lax.ppermute only.
A program may use at most 128 MiB of HBM per device.

```python
import math
import jax
import jax.numpy as jnp
from jax import lax

WIDTH = 256
STEPS = 2
PLANES = 8
TILES = 128
TOTAL = 2048


def block_levels(key, shape, shards, smallest, largest):
    def one(dim, shards_of):
        draws = jax.random.uniform(jax.random.fold_in(jax.random.fold_in(key, 6), dim), (shards_of,), jnp.float32, smallest / len(shards), largest / len(shards))
        return jnp.repeat(jnp.exp(draws), shape[dim] // shards_of).reshape((-1,) + (1,) * (len(shape) - dim - 1))

    loudness = one(*shards[0])
    for cut in shards[1:]:
        loudness = loudness * one(*cut)
    return loudness


def noise(key, shape, spread, reach, cuts=(), held_as=jnp.bfloat16):
    gain = block_levels(key, shape, cuts, -0.22, 0.18) if cuts else 1.0
    values = jax.random.normal(key, shape, jnp.float32) * spread * gain
    return jnp.minimum(jnp.maximum(values, -reach), reach).astype(held_as)


def setup_inputs(seed: int = 0) -> dict:
    splits = jax.random.split(jax.random.key(seed), 5)
    fields = noise(splits[0], (2, PLANES, TILES, WIDTH, WIDTH), 0.7, 5.0, ((1, 8), (2, 16)), jnp.float32)
    amplitudes = jnp.clip(jnp.exp(math.log(3.0) - 2.3025851 * jax.random.uniform(splits[1], (PLANES, TILES, WIDTH, WIDTH), jnp.float32) ** block_levels(splits[1], (PLANES, TILES, WIDTH, WIDTH), ((0, 8), (1, 16)), -0.2, 0.2)), 0.3, 3.0)
    pupil = noise(splits[2], (2, WIDTH, WIDTH), 0.7, 4.0, (), jnp.float32)
    distances = jnp.clip(5.0 + 35.0 * jax.random.uniform(splits[3], (PLANES,), jnp.float32) ** block_levels(splits[3], (PLANES,), ((0, 8),), -0.2, 0.2), 5.0, 40.0)
    return {"fields": fields, "amplitudes": amplitudes, "pupil": pupil, "distances": distances}


def dft_tables(length):
    index = jnp.arange(length, dtype=jnp.int32)
    product = index[:, None] * index[None, :] % length
    angle = product.astype(jnp.float32) * (2.0 * math.pi / length)
    factor = 1.0 / math.sqrt(length)
    return (jnp.cos(angle) * factor, -jnp.sin(angle) * factor)

def transfer_phase(length):
    index = jnp.arange(length, dtype=jnp.int32)
    freq = ((index + length // 2) % length - length // 2).astype(jnp.float32) / length
    return math.pi * (freq[:, None] ** 2 + freq[None, :] ** 2)

def left_product(mat_re, mat_im, tile_re, tile_im):

    def single(fourier_matrix, image_patch):
        return jnp.einsum('im,qmy->qiy', fourier_matrix, image_patch, precision=lax.Precision.HIGHEST)
    return (single(mat_re, tile_re) - single(mat_im, tile_im), single(mat_re, tile_im) + single(mat_im, tile_re))

def right_product(tile_re, tile_im, mat_re, mat_im):

    def single(image_patch, fourier_matrix):
        return jnp.einsum('zus,sg->zug', image_patch, fourier_matrix, precision=lax.Precision.HIGHEST)
    return (single(tile_re, mat_re) - single(tile_im, mat_im), single(tile_re, mat_im) + single(tile_im, mat_re))

def propagate(pupil, field, distance, cosine_lookup, sin_table, phase):
    spectrum_real, spec_im = left_product(cosine_lookup, sin_table, field[0], field[1])
    spectrum_real, spec_im = right_product(spectrum_real, spec_im, cosine_lookup, sin_table)
    kern_re = jnp.cos(distance * phase)
    kern_im = jnp.sin(distance * phase)
    filt_re = pupil[0] * kern_re - pupil[1] * kern_im
    filt_im = pupil[0] * kern_im + pupil[1] * kern_re
    prod_re = spectrum_real * filt_re - spec_im * filt_im
    prod_im = spectrum_real * filt_im + spec_im * filt_re
    out_re, out_im = left_product(cosine_lookup, -sin_table, prod_re, prod_im)
    return right_product(out_re, out_im, cosine_lookup, -sin_table)

def residual_error(pupil, field, distance, amps, cosine_lookup, sin_table, phase, factor):
    wave_re, wave_im = propagate(pupil, field, distance, cosine_lookup, sin_table, phase)
    modulus = jnp.sqrt(wave_re * wave_re + wave_im * wave_im + 0.25)
    loss = jnp.sum((modulus - amps) ** 2) * factor
    return (loss, (wave_re, wave_im, modulus))

def reference(fields, amplitudes, pupil, distances):
    length = pupil.shape[-1]
    cosine_lookup, sin_table = dft_tables(length)
    phase = transfer_phase(length)
    factor = 1.0 / math.sqrt(TOTAL)
    gradient_fn = jax.grad(residual_error, has_aux=True)
    state = fields
    total = jnp.zeros(pupil.shape, jnp.float32)
    for sweep_step in range(STEPS):
        planes_new = []
        for measured_target in range(PLANES):
            source = (measured_target - 1) % PLANES
            amps = amplitudes[measured_target]
            grad, (wave_re, wave_im, modulus) = gradient_fn(pupil, state[:, source], distances[source], amps, cosine_lookup, sin_table, phase, factor)
            total = total + grad
            planes_new.append(jnp.stack([amps * wave_re / modulus, amps * wave_im / modulus]))
        state = jnp.stack(planes_new, axis=1)
    return (state, total)
```

```python
import math

import jax
import jax.numpy as jnp
import numpy as np
from jax import lax
from jax.experimental import pallas as pl
from jax.experimental.pallas import tpu as pltpu
from jax.sharding import PartitionSpec as P

STEPS = 2
WIDTH = 256
HALF = WIDTH // 2
AXES = ("tile", "plane")
F32, BF16 = jnp.float32, jnp.bfloat16

ROUTES = ("ahead", "ahead", "ahead", "ahead", "both", "back", "back", "back")


def plane_pairs(steps, count):
    return [(source, (source + steps) % count) for source in range(count)]


def back_pairs(count, ring):
    return [(p, p // ring * ring + (p % ring + ring - 1) % ring) for p in range(count)]


def back_rest(count, ring):
    return [(p // ring * ring + (p % ring + ring - 1) % ring, (p + 2) % count) for p in range(count)]


def order():
    return np.concatenate([np.arange(0, WIDTH, 2), np.arange(1, WIDTH, 2)])


def dft_halves():
    j, k = np.arange(HALF)[:, None], np.arange(HALF)[None, :]
    halves = []
    for odd in (0, 1):
        angle = -2.0 * np.pi * (j * (2 * k + odd) % WIDTH) / WIDTH
        re, im = np.cos(angle) / math.sqrt(WIDTH), np.sin(angle) / math.sqrt(WIDTH)
        halves.append(np.block([[re, im], [-im, re]]))
    return np.stack(halves)


def dft_tables():
    plain = dft_halves()
    full = np.concatenate([plain, plain.transpose(0, 2, 1)])
    high = full.astype(BF16)
    low = (full - high.astype(np.float64)).astype(BF16)
    return np.stack([high, low])


def transfer_phase():
    index = np.arange(WIDTH)
    freq = (((index + HALF) % WIDTH - HALF) / WIDTH)[order()]
    return (np.pi * (freq[:, None] ** 2 + freq[None, :] ** 2)).astype(np.float32)


def shuffle():
    return np.eye(WIDTH, dtype=np.float32)[order()]


def split(x):
    high = x.astype(BF16)
    return high, (x - high.astype(F32)).astype(BF16)


def dot(a, b):
    return jnp.dot(a, b, preferred_element_type=F32)


def right(t, tables, k):
    high, low = split(t)
    return dot(high, tables[0, k]) + (dot(low, tables[0, k]) + dot(high, tables[1, k]))


def left(tables, k, t):
    high, low = split(t)
    return dot(tables[0, k], high) + (dot(tables[0, k], low) + dot(tables[1, k], high))


def forward(re, im, tables):
    a = [re[:, :HALF], im[:, :HALF]]
    b = [re[:, HALF:], im[:, HALF:]]
    even = right(jnp.concatenate([a[0] + b[0], a[1] + b[1]], 1), tables, 0)
    odd = right(jnp.concatenate([a[0] - b[0], a[1] - b[1]], 1), tables, 1)
    re = jnp.concatenate([even[:, :HALF], odd[:, :HALF]], 1)
    im = jnp.concatenate([even[:, HALF:], odd[:, HALF:]], 1)
    a = [re[:HALF], im[:HALF]]
    b = [re[HALF:], im[HALF:]]
    even = left(tables, 2, jnp.concatenate([a[0] + b[0], a[1] + b[1]], 0))
    odd = left(tables, 3, jnp.concatenate([a[0] - b[0], a[1] - b[1]], 0))
    return (jnp.concatenate([even[:HALF], odd[:HALF]], 0), jnp.concatenate([even[HALF:], odd[HALF:]], 0))


def inverse(re, im, tables):
    even = left(tables, 0, jnp.concatenate([re[:HALF], im[:HALF]], 0))
    odd = left(tables, 1, jnp.concatenate([re[HALF:], im[HALF:]], 0))
    up, down = even + odd, even - odd
    re = jnp.concatenate([up[:HALF], down[:HALF]], 0)
    im = jnp.concatenate([up[HALF:], down[HALF:]], 0)
    even = right(jnp.concatenate([re[:, :HALF], im[:, :HALF]], 1), tables, 2)
    odd = right(jnp.concatenate([re[:, HALF:], im[:, HALF:]], 1), tables, 3)
    up, down = even + odd, even - odd
    return (
        jnp.concatenate([up[:, :HALF], down[:, :HALF]], 1),
        jnp.concatenate([up[:, HALF:], down[:, HALF:]], 1),
    )


def product(a_re, a_im, b_re, b_im):
    return a_re * b_re - a_im * b_im, a_re * b_im + a_im * b_re


def product_conj(a_re, a_im, b_re, b_im):
    return a_re * b_re + a_im * b_im, a_im * b_re - a_re * b_im


def constrained(u_re, u_im, amps):
    scale = amps * lax.rsqrt(u_re * u_re + u_im * u_im + 0.25)
    return u_re * scale, u_im * scale


def first_kernel(f_ref, a_ref, q_ref, tables, g_ref, spec_ref, grad_ref):
    s_re, s_im = forward(f_ref[0, 0], f_ref[1, 0], tables)
    p_re, p_im = product(s_re, s_im, q_ref[0], q_ref[1])
    n_re, n_im = constrained(*inverse(p_re, p_im, tables), a_ref[0])
    n_re, n_im = forward(n_re, n_im, tables)
    spec_ref[0, 0] = n_re
    spec_ref[1, 0] = n_im
    g_re, g_im = product_conj(p_re - n_re, p_im - n_im, s_re, s_im)
    grad_ref[0] = g_ref[0] + g_re
    grad_ref[1] = g_ref[1] + g_im


def second_kernel(s_ref, a_ref, q_ref, tables, g_ref, *rest):
    out_ref, grad_ref = rest[-2:]
    s_re, s_im = s_ref[0, 0], s_ref[1, 0]
    u_re, u_im = inverse(*product(s_re, s_im, q_ref[0], q_ref[1]), tables)
    n_re, n_im = constrained(u_re, u_im, a_ref[0])
    out_ref[0, 0] = n_re
    out_ref[1, 0] = n_im
    w_re, w_im = forward(u_re - n_re, u_im - n_im, tables)
    g_re, g_im = product_conj(w_re, w_im, s_re, s_im)
    grad_ref[0] = g_ref[0] + g_re
    grad_ref[1] = g_ref[1] + g_im


def tile_spec(shape, at):
    if len(shape) == 4:
        return pl.BlockSpec((2, 1, WIDTH, WIDTH), lambda i: (0, at, 0, 0))
    return pl.BlockSpec((1, WIDTH, WIDTH), lambda i: (at, 0, 0))


def whole(shape):
    return pl.BlockSpec(shape, lambda i: (0,) * len(shape))


COST = pl.CostEstimate(flops=2_000_000_000, bytes_accessed=4_000_000, transcendentals=0)
PARAMS = pltpu.CompilerParams(vmem_limit_bytes=40 * 1024 * 1024)
PAIR = (2, WIDTH, WIDTH)


def first_step(f, f_at, amps, a_at, q, tables, grad):
    return pl.pallas_call(
        first_kernel,
        grid=(1,),
        in_specs=[tile_spec(f.shape, f_at), tile_spec(amps.shape, a_at), whole(PAIR), whole(tables.shape), whole(PAIR)],
        out_specs=[tile_spec((2, 1, WIDTH, WIDTH), 0), whole(PAIR)],
        out_shape=[jax.ShapeDtypeStruct((2, 1, WIDTH, WIDTH), F32), jax.ShapeDtypeStruct(PAIR, F32)],
        input_output_aliases={4: 1},
        compiler_params=PARAMS,
        cost_estimate=COST,
        name="first_step",
    )(f, amps, q, tables, grad)


def second_step(spectrum, amps, a_at, q, tables, grad, out, out_at, count):
    shape = (2, count, WIDTH, WIDTH)
    more = [] if out is None else [out]
    return pl.pallas_call(
        second_kernel,
        grid=(1,),
        in_specs=[tile_spec(spectrum.shape, 0), tile_spec(amps.shape, a_at), whole(PAIR), whole(tables.shape), whole(PAIR)]
        + [pl.BlockSpec(memory_space=pl.ANY) for _ in more],
        out_specs=[tile_spec(shape, out_at), whole(PAIR)],
        out_shape=[jax.ShapeDtypeStruct(shape, F32), jax.ShapeDtypeStruct(PAIR, F32)],
        input_output_aliases={4: 1, 5: 0} if more else {4: 1},
        compiler_params=PARAMS,
        cost_estimate=COST,
        name="second_step",
    )(spectrum, amps, q, tables, grad, *more)


def core_pairs(tiles, planes):
    return [(t * planes + p, (t ^ 1) * planes + p) for t in range(tiles) for p in range(planes)]


def summed(grad):
    tiles, planes = lax.axis_size("tile"), lax.axis_size("plane")
    groups = [[t * planes + p for t in range(core, tiles, 2) for p in range(planes)] for core in (0, 1)]
    members = len(groups[0])
    core = lax.axis_index("tile") % 2
    parts = grad.reshape(2, WIDTH, 2, HALF).transpose(0, 2, 1, 3)
    mine, others = jnp.where(core == 0, parts[0], parts[1]), jnp.where(core == 0, parts[1], parts[0])
    mine = mine + lax.ppermute(others, AXES, core_pairs(tiles, planes))
    mine = mine.reshape(members, -1, HALF)
    mine = lax.all_to_all(mine, AXES, 0, 0, tiled=True, axis_index_groups=groups).sum(0)
    mine = jnp.broadcast_to(mine[None], (members, *mine.shape))
    mine = lax.all_to_all(mine, AXES, 0, 0, tiled=True, axis_index_groups=groups).reshape(2, WIDTH, HALF)
    others = lax.ppermute(mine, AXES, core_pairs(tiles, planes))
    total = jnp.where(core == 0, jnp.stack([mine, others]), jnp.stack([others, mine]))
    return total.transpose(0, 2, 1, 3).reshape(2, WIDTH, WIDTH)


def turned(distance):
    angle = distance * jnp.asarray(transfer_phase())
    return jnp.cos(angle), jnp.sin(angle)


def body(ring, fields, amplitudes, pupil, distances):
    planes, tiles_all = lax.axis_size("plane"), lax.axis_size("tile")
    fields, amps = fields[:, 0], amplitudes[0]
    count = amps.shape[0]
    factor = 1.0 / math.sqrt(STEPS * planes * tiles_all * count)
    tables = jnp.asarray(dft_tables())
    mix = jnp.asarray(shuffle())

    def sent(value, pairs):
        return lax.ppermute(value, "plane", pairs)

    ahead, behind = plane_pairs(1, planes), plane_pairs(-1, planes)
    distance_before = sent(distances, ahead)
    at_home = [t for t in range(count) if ROUTES[t] != "ahead"]
    on_ahead = [t for t in range(count) if ROUTES[t] == "ahead"]
    moved = {t: sent(fields[:, t : t + 1], ahead) for t in on_ahead}
    amps_next = {t: sent(amps[t : t + 1], behind) for t in at_home}

    shuffled = jnp.einsum("ij,cjk,lk->cil", mix, pupil, mix, precision=lax.Precision.HIGHEST)
    turn_before, turn_here = turned(distance_before[0]), turned(distances[0])
    q_before = jnp.stack(product(shuffled[0], shuffled[1], *turn_before))
    q_here = jnp.stack(product(shuffled[0], shuffled[1], *turn_here))
    grad_before = jnp.zeros(PAIR, F32)
    grad_here = jnp.zeros(PAIR, F32)

    spectra = {}
    for n in range(max(len(at_home), len(on_ahead))):
        if n < len(at_home):
            t = at_home[n]
            spectrum, grad_here = first_step(fields, t, amps_next[t], 0, q_here, tables, grad_here)
            if ROUTES[t] == "both":
                spectra[t] = sent(spectrum, plane_pairs(2, planes))
            else:
                spectra[t] = sent(sent(spectrum, back_pairs(planes, ring)), back_rest(planes, ring))
        if n < len(on_ahead):
            t = on_ahead[n]
            spectrum, grad_before = first_step(moved[t], 0, amps, t, q_before, tables, grad_before)
            spectra[t] = sent(spectrum, ahead)
    out = None
    for n in range(max(len(at_home), len(on_ahead))):
        for some in (at_home, on_ahead):
            if n < len(some):
                t = some[n]
                out, grad_before = second_step(spectra[t], amps, t, q_before, tables, grad_before, out, t, count)

    a, b = product_conj(*grad_before, *turn_before), product_conj(*grad_here, *turn_here)
    grad = jnp.stack([a[0] + b[0], a[1] + b[1]]) * (2.0 * factor)
    grad = jnp.einsum("ji,cjk,kl->cil", mix, grad, mix, precision=lax.Precision.HIGHEST)
    return (out[:, None], summed(grad))


def solution(mesh):
    placed = (P(None, "plane", "tile", None, None), P("plane", "tile", None, None), P(), P("plane"))
    ring = mesh.shape["plane"] // 2

    def step(*args):
        return body(ring, *args)

    return jax.shard_map(
        step,
        mesh=mesh,
        in_specs=placed,
        out_specs=(P(None, "plane", "tile", None, None), P()),
        check_vma=False,
    )
```

```python
import math

import jax
import jax.numpy as jnp
import numpy as np
from jax import lax
from jax.experimental import pallas as pl
from jax.experimental.pallas import tpu as pltpu
from jax.sharding import PartitionSpec as P

STEPS = 2
WIDTH = 256
HALF = WIDTH // 2
AXES = ("tile", "plane")
F32, BF16 = jnp.float32, jnp.bfloat16


def plane_pairs(steps, count):
    return [(source, (source + steps) % count) for source in range(count)]


def back_place(p, count, ring):
    return (p + 2) % count // ring * ring + (p % ring + ring - 1) % ring


def back_pairs(count, ring):
    return [(p, back_place(p, count, ring)) for p in range(count)]


def rest_pairs(count, ring):
    return [(back_place(p, count, ring), (p + 2) % count) for p in range(count)]


def order():
    return np.concatenate([np.arange(0, WIDTH, 2), np.arange(1, WIDTH, 2)])


def dft_halves():
    j, k = np.arange(HALF)[:, None], np.arange(HALF)[None, :]
    halves = []
    for odd in (0, 1):
        angle = -2.0 * np.pi * (j * (2 * k + odd) % WIDTH) / WIDTH
        re, im = np.cos(angle) / math.sqrt(WIDTH), np.sin(angle) / math.sqrt(WIDTH)
        halves.append(np.block([[re, im], [-im, re]]))
    return np.stack(halves)


def dft_tables():
    plain = dft_halves()
    full = np.concatenate([plain, plain.transpose(0, 2, 1)])
    high = full.astype(BF16)
    low = (full - high.astype(np.float64)).astype(BF16)
    return np.stack([high, low])


def transfer_phase():
    index = np.arange(WIDTH)
    freq = (((index + HALF) % WIDTH - HALF) / WIDTH)[order()]
    return (np.pi * (freq[:, None] ** 2 + freq[None, :] ** 2)).astype(np.float32)


def shuffle():
    return np.eye(WIDTH, dtype=np.float32)[order()]


def split(x):
    high = x.astype(BF16)
    return high, (x - high.astype(F32)).astype(BF16)


def dot(a, b):
    return jnp.dot(a, b, preferred_element_type=F32)


def right(t, tables, k):
    high, low = split(t)
    return dot(high, tables[0, k]) + (dot(low, tables[0, k]) + dot(high, tables[1, k]))


def left(tables, k, t):
    high, low = split(t)
    return dot(tables[0, k], high) + (dot(tables[0, k], low) + dot(tables[1, k], high))


def forward(re, im, tables):
    a = [re[:, :HALF], im[:, :HALF]]
    b = [re[:, HALF:], im[:, HALF:]]
    even = right(jnp.concatenate([a[0] + b[0], a[1] + b[1]], 1), tables, 0)
    odd = right(jnp.concatenate([a[0] - b[0], a[1] - b[1]], 1), tables, 1)
    re = jnp.concatenate([even[:, :HALF], odd[:, :HALF]], 1)
    im = jnp.concatenate([even[:, HALF:], odd[:, HALF:]], 1)
    a = [re[:HALF], im[:HALF]]
    b = [re[HALF:], im[HALF:]]
    even = left(tables, 2, jnp.concatenate([a[0] + b[0], a[1] + b[1]], 0))
    odd = left(tables, 3, jnp.concatenate([a[0] - b[0], a[1] - b[1]], 0))
    return (jnp.concatenate([even[:HALF], odd[:HALF]], 0), jnp.concatenate([even[HALF:], odd[HALF:]], 0))


def inverse(re, im, tables):
    even = left(tables, 0, jnp.concatenate([re[:HALF], im[:HALF]], 0))
    odd = left(tables, 1, jnp.concatenate([re[HALF:], im[HALF:]], 0))
    up, down = even + odd, even - odd
    re = jnp.concatenate([up[:HALF], down[:HALF]], 0)
    im = jnp.concatenate([up[HALF:], down[HALF:]], 0)
    even = right(jnp.concatenate([re[:, :HALF], im[:, :HALF]], 1), tables, 2)
    odd = right(jnp.concatenate([re[:, HALF:], im[:, HALF:]], 1), tables, 3)
    up, down = even + odd, even - odd
    return (
        jnp.concatenate([up[:, :HALF], down[:, :HALF]], 1),
        jnp.concatenate([up[:, HALF:], down[:, HALF:]], 1),
    )


def product(a_re, a_im, b_re, b_im):
    return a_re * b_re - a_im * b_im, a_re * b_im + a_im * b_re


def product_conj(a_re, a_im, b_re, b_im):
    return a_re * b_re + a_im * b_im, a_im * b_re - a_re * b_im


def constrained(u_re, u_im, amps):
    scale = amps * lax.rsqrt(u_re * u_re + u_im * u_im + 0.25)
    return u_re * scale, u_im * scale


def first_kernel(f_ref, a_ref, q_ref, tables, g_ref, *rest):
    spec_ref, grad_ref = rest[-3:-1]
    s_re, s_im = forward(f_ref[0, 0], f_ref[1, 0], tables)
    p_re, p_im = product(s_re, s_im, q_ref[0], q_ref[1])
    n_re, n_im = constrained(*inverse(p_re, p_im, tables), a_ref[0])
    n_re, n_im = forward(n_re, n_im, tables)
    spec_ref[0, 0] = n_re
    spec_ref[1, 0] = n_im
    add(g_ref, grad_ref, *product_conj(p_re - n_re, p_im - n_im, s_re, s_im))


def second_kernel(s_ref, a_ref, q_ref, tables, g_ref, *rest):
    out_ref, grad_ref = rest[-3:-1]
    s_re, s_im = s_ref[0, 0], s_ref[1, 0]
    u_re, u_im = inverse(*product(s_re, s_im, q_ref[0], q_ref[1]), tables)
    n_re, n_im = constrained(u_re, u_im, a_ref[0])
    out_ref[0, 0] = n_re
    out_ref[1, 0] = n_im
    w_re, w_im = forward(u_re - n_re, u_im - n_im, tables)
    add(g_ref, grad_ref, *product_conj(w_re, w_im, s_re, s_im))


def add(g_ref, grad_ref, g_re, g_im):
    @pl.when(pl.program_id(0) == 0)
    def _():
        grad_ref[...] = g_ref[...]

    grad_ref[0] += g_re
    grad_ref[1] += g_im


def tile_spec(shape, at):
    if len(shape) == 4:
        return pl.BlockSpec((2, 1, WIDTH, WIDTH), lambda i: (0, at + i, 0, 0))
    return pl.BlockSpec((1, WIDTH, WIDTH), lambda i: (at + i, 0, 0))


def whole(shape):
    return pl.BlockSpec(shape, lambda i: (0,) * len(shape))


ANY = pl.BlockSpec(memory_space=pl.ANY)
PAIR = (2, WIDTH, WIDTH)


def step_call(kernel, x, x_at, amps, a_at, q, tables, grad, token, tiles, out, out_at, out_tiles, after, weight, name):
    shape = (2, out_tiles, WIDTH, WIDTH)
    more = [token, *([] if out is None else [out]), *after]
    aliases = {4: 1, 5: 2} if out is None else {4: 1, 5: 2, 6: 0}
    return pl.pallas_call(
        kernel,
        grid=(tiles,),
        in_specs=[tile_spec(x.shape, x_at), tile_spec(amps.shape, a_at), whole(PAIR), whole(tables.shape), whole(PAIR)]
        + [ANY for _ in more],
        out_specs=[tile_spec(shape, out_at), whole(PAIR), ANY],
        out_shape=[
            jax.ShapeDtypeStruct(shape, F32),
            jax.ShapeDtypeStruct(PAIR, F32),
            jax.ShapeDtypeStruct(token.shape, F32),
        ],
        input_output_aliases=aliases,
        compiler_params=pltpu.CompilerParams(vmem_limit_bytes=40 * 1024 * 1024),
        cost_estimate=pl.CostEstimate(flops=int(weight * 1_000_000_000), bytes_accessed=tiles * 400_000, transcendentals=0),
        name=name,
    )(x, amps, q, tables, grad, *more)


def finish_kernel(a_ref, b_ref, ta_re, ta_im, tb_re, tb_im, mix, factor_ref, out_ref):
    a = product_conj(a_ref[0], a_ref[1], ta_re[...], ta_im[...])
    b = product_conj(b_ref[0], b_ref[1], tb_re[...], tb_im[...])
    for part in (0, 1):
        x = (a[part] + b[part]) * factor_ref[0]
        x = sum(dot(mix[1], piece) for piece in pieces(x))
        x = sum(dot(piece, mix[0]) for piece in pieces(x))
        out_ref[part, 0] = x[:, :HALF]
        out_ref[part, 1] = x[:, HALF:]


def pieces(x):
    high = x.astype(BF16)
    x = x - high.astype(F32)
    middle = x.astype(BF16)
    return high, middle, (x - middle.astype(F32)).astype(BF16)


def finished(grad_a, grad_b, turn_a, turn_b, mix, factor):
    vmem = pl.BlockSpec(memory_space=pltpu.VMEM)
    both = jnp.asarray(np.stack([mix, mix.T]).astype(BF16))
    return pl.pallas_call(
        finish_kernel,
        in_specs=[vmem] * 7 + [pl.BlockSpec(memory_space=pltpu.SMEM)],
        out_specs=vmem,
        out_shape=jax.ShapeDtypeStruct((2, 2, WIDTH, HALF), F32),
        compiler_params=pltpu.CompilerParams(vmem_limit_bytes=40 * 1024 * 1024),
        name="finish",
    )(grad_a, grad_b, *turn_a, *turn_b, both, jnp.full((1,), factor, F32))


def summed(parts):
    members = lax.axis_size("tile") * lax.axis_size("plane")
    mine = parts.reshape(members, -1, HALF)
    mine = lax.all_to_all(mine, AXES, 0, 0, tiled=True).sum(0)
    mine = jnp.broadcast_to(mine[None], (members, *mine.shape))
    total = lax.all_to_all(mine, AXES, 0, 0, tiled=True).reshape(2, 2, WIDTH, HALF)
    return total.transpose(0, 2, 1, 3).reshape(2, WIDTH, WIDTH)


def turned(distance):
    angle = distance * jnp.asarray(transfer_phase())
    return jnp.cos(angle), jnp.sin(angle)


def body(ring, fields, amplitudes, pupil, distances):
    planes, tiles_all = lax.axis_size("plane"), lax.axis_size("tile")
    fields, amps = fields[:, 0], amplitudes[0]
    count = amps.shape[0]
    factor = 1.0 / math.sqrt(STEPS * planes * tiles_all * count)
    tables = jnp.asarray(dft_tables())
    mix = shuffle()

    def sent(value, pairs):
        return lax.ppermute(value, "plane", pairs)

    ahead, behind = plane_pairs(1, planes), plane_pairs(-1, planes)
    back, rest = back_pairs(planes, ring), rest_pairs(planes, ring)

    amps_45 = sent(amps[4:6], behind)
    fields_01 = sent(fields[:, 0:2], ahead)
    distance_before = sent(distances, ahead)
    shuffled = jnp.einsum("ij,cjk,lk->cil", mix, pupil, mix, precision=lax.Precision.HIGHEST)
    turn_before, turn_here = turned(distance_before[0]), turned(distances[0])
    q_before = jnp.stack(product(shuffled[0], shuffled[1], *turn_before))
    q_here = jnp.stack(product(shuffled[0], shuffled[1], *turn_here))
    later_amps, later_fields, q_before = lax.optimization_barrier((amps, fields, q_before))
    amps_67 = sent(later_amps[6:8], behind)
    fields_23 = sent(later_fields[:, 2:4], ahead)

    grads = {"before": jnp.zeros(PAIR, F32), "here": jnp.zeros(PAIR, F32)}
    filters = {"before": q_before, "here": q_here}
    token = jnp.zeros((8, 128), F32)

    def first(which, x, x_at, a, a_at, tiles, weight, after=()):
        nonlocal token
        result, grads[which], token = step_call(
            first_kernel, x, x_at, a, a_at, filters[which], tables, grads[which], token, tiles, None, 0, tiles, after, weight, "first_step")
        return result

    out = None

    def second(x, at, tiles, weight):
        nonlocal token, out
        out, grads["before"], token = step_call(
            second_kernel, x, 0, amps, at, filters["before"], tables, grads["before"], token, tiles, out, at, count, (), weight, "second_step")

    weights = [10, 20, 20, 20, 0.1, 3, 3]
    s_45 = sent(first("here", fields, 4, amps_45, 0, 2, weights[0]), back)
    s_6 = sent(first("here", fields, 6, amps_67, 0, 1, weights[1]), back)
    s_01 = sent(first("before", fields_01, 0, amps, 0, 2, weights[2]), ahead)
    s_7 = sent(first("here", fields, 7, amps_67, 1, 1, weights[3]), plane_pairs(2, planes))
    s_23 = sent(first("before", fields_23, 0, amps, 2, 2, weights[4]), ahead)
    s_45 = sent(s_45, rest)
    s_6 = sent(s_6, rest)
    second(s_01, 0, 2, weights[6])
    second(s_7, 7, 1, weights[6])
    second(s_45, 4, 2, weights[6])
    second(s_6, 6, 1, weights[6])
    second(s_23, 2, 2, weights[5])

    parts = finished(grads["before"], grads["here"], turn_before, turn_here, mix, 2.0 * factor)
    return (out[:, None], summed(parts))


def solution(mesh):
    placed = (P(None, "plane", "tile", None, None), P("plane", "tile", None, None), P(), P("plane"))
    ring = mesh.shape["plane"] // 2

    def step(*args):
        return body(ring, *args)

    return jax.shard_map(
        step,
        mesh=mesh,
        in_specs=placed,
        out_specs=(P(None, "plane", "tile", None, None), P()),
        check_vma=False,
    )
```

```python
import math

import jax
import jax.numpy as jnp
import numpy as np
from jax import lax
from jax.experimental import pallas as pl
from jax.experimental.pallas import tpu as pltpu
from jax.sharding import PartitionSpec as P

STEPS = 2
WIDTH = 256
HALF = WIDTH // 2
AXES = ("tile", "plane")
F32, BF16 = jnp.float32, jnp.bfloat16


def plane_pairs(steps, count):
    return [(source, (source + steps) % count) for source in range(count)]


def back_place(p, count, ring):
    return (p + 2) % count // ring * ring + (p % ring + ring - 1) % ring


def back_pairs(count, ring):
    return [(p, back_place(p, count, ring)) for p in range(count)]


def rest_pairs(count, ring):
    return [(back_place(p, count, ring), (p + 2) % count) for p in range(count)]


def order():
    return np.concatenate([np.arange(0, WIDTH, 2), np.arange(1, WIDTH, 2)])


def dft_halves():
    j, k = np.arange(HALF)[:, None], np.arange(HALF)[None, :]
    halves = []
    for odd in (0, 1):
        angle = -2.0 * np.pi * (j * (2 * k + odd) % WIDTH) / WIDTH
        re, im = np.cos(angle) / math.sqrt(WIDTH), np.sin(angle) / math.sqrt(WIDTH)
        halves.append(np.block([[re, im], [-im, re]]))
    return np.stack(halves)


def dft_tables():
    plain = dft_halves()
    full = np.concatenate([plain, plain.transpose(0, 2, 1)])
    high = full.astype(BF16)
    low = (full - high.astype(np.float64)).astype(BF16)
    return np.stack([high, low])


def transfer_phase():
    index = np.arange(WIDTH)
    freq = (((index + HALF) % WIDTH - HALF) / WIDTH)[order()]
    return (np.pi * (freq[:, None] ** 2 + freq[None, :] ** 2)).astype(np.float32)


def shuffle():
    return np.eye(WIDTH, dtype=np.float32)[order()]


def split(x):
    high = x.astype(BF16)
    return high, (x - high.astype(F32)).astype(BF16)


def dot(a, b):
    return jnp.dot(a, b, preferred_element_type=F32)


def right(t, tables, k):
    high, low = split(t)
    return dot(high, tables[0, k]) + (dot(low, tables[0, k]) + dot(high, tables[1, k]))


def left(tables, k, t):
    high, low = split(t)
    return dot(tables[0, k], high) + (dot(tables[0, k], low) + dot(tables[1, k], high))


def forward(re, im, tables):
    a = [re[:, :HALF], im[:, :HALF]]
    b = [re[:, HALF:], im[:, HALF:]]
    even = right(jnp.concatenate([a[0] + b[0], a[1] + b[1]], 1), tables, 0)
    odd = right(jnp.concatenate([a[0] - b[0], a[1] - b[1]], 1), tables, 1)
    re = jnp.concatenate([even[:, :HALF], odd[:, :HALF]], 1)
    im = jnp.concatenate([even[:, HALF:], odd[:, HALF:]], 1)
    a = [re[:HALF], im[:HALF]]
    b = [re[HALF:], im[HALF:]]
    even = left(tables, 2, jnp.concatenate([a[0] + b[0], a[1] + b[1]], 0))
    odd = left(tables, 3, jnp.concatenate([a[0] - b[0], a[1] - b[1]], 0))
    return (jnp.concatenate([even[:HALF], odd[:HALF]], 0), jnp.concatenate([even[HALF:], odd[HALF:]], 0))


def inverse(re, im, tables):
    even = left(tables, 0, jnp.concatenate([re[:HALF], im[:HALF]], 0))
    odd = left(tables, 1, jnp.concatenate([re[HALF:], im[HALF:]], 0))
    up, down = even + odd, even - odd
    re = jnp.concatenate([up[:HALF], down[:HALF]], 0)
    im = jnp.concatenate([up[HALF:], down[HALF:]], 0)
    even = right(jnp.concatenate([re[:, :HALF], im[:, :HALF]], 1), tables, 2)
    odd = right(jnp.concatenate([re[:, HALF:], im[:, HALF:]], 1), tables, 3)
    up, down = even + odd, even - odd
    return (
        jnp.concatenate([up[:, :HALF], down[:, :HALF]], 1),
        jnp.concatenate([up[:, HALF:], down[:, HALF:]], 1),
    )


def product(a_re, a_im, b_re, b_im):
    return a_re * b_re - a_im * b_im, a_re * b_im + a_im * b_re


def product_conj(a_re, a_im, b_re, b_im):
    return a_re * b_re + a_im * b_im, a_im * b_re - a_re * b_im


def constrained(u_re, u_im, amps):
    scale = amps * lax.rsqrt(u_re * u_re + u_im * u_im + 0.25)
    return u_re * scale, u_im * scale


def first_kernel(f_ref, a_ref, q_ref, tables, g_ref, *rest):
    spec_ref, grad_ref = rest[-3:-1]
    s_re, s_im = forward(f_ref[0, 0], f_ref[1, 0], tables)
    p_re, p_im = product(s_re, s_im, q_ref[0], q_ref[1])
    n_re, n_im = constrained(*inverse(p_re, p_im, tables), a_ref[0])
    n_re, n_im = forward(n_re, n_im, tables)
    spec_ref[0, 0] = n_re
    spec_ref[1, 0] = n_im
    add(g_ref, grad_ref, *product_conj(p_re - n_re, p_im - n_im, s_re, s_im))


def second_kernel(s_ref, a_ref, q_ref, tables, g_ref, *rest):
    out_ref, grad_ref = rest[-3:-1]
    s_re, s_im = s_ref[0, 0], s_ref[1, 0]
    u_re, u_im = inverse(*product(s_re, s_im, q_ref[0], q_ref[1]), tables)
    n_re, n_im = constrained(u_re, u_im, a_ref[0])
    out_ref[0, 0] = n_re
    out_ref[1, 0] = n_im
    w_re, w_im = forward(u_re - n_re, u_im - n_im, tables)
    add(g_ref, grad_ref, *product_conj(w_re, w_im, s_re, s_im))


def add(g_ref, grad_ref, g_re, g_im):
    @pl.when(pl.program_id(0) == 0)
    def _():
        grad_ref[...] = g_ref[...]

    grad_ref[0] += g_re
    grad_ref[1] += g_im


def tile_spec(shape, at):
    if len(shape) == 4:
        return pl.BlockSpec((2, 1, WIDTH, WIDTH), lambda i: (0, at + i, 0, 0))
    return pl.BlockSpec((1, WIDTH, WIDTH), lambda i: (at + i, 0, 0))


def whole(shape):
    return pl.BlockSpec(shape, lambda i: (0,) * len(shape))


ANY = pl.BlockSpec(memory_space=pl.ANY)
PAIR = (2, WIDTH, WIDTH)


def step_call(kernel, x, x_at, amps, a_at, q, tables, grad, token, tiles, out, out_at, out_tiles, after, weight, name):
    shape = (2, out_tiles, WIDTH, WIDTH)
    more = [token, *([] if out is None else [out]), *after]
    aliases = {4: 1, 5: 2} if out is None else {4: 1, 5: 2, 6: 0}
    return pl.pallas_call(
        kernel,
        grid=(tiles,),
        in_specs=[tile_spec(x.shape, x_at), tile_spec(amps.shape, a_at), whole(PAIR), whole(tables.shape), whole(PAIR)]
        + [ANY for _ in more],
        out_specs=[tile_spec(shape, out_at), whole(PAIR), ANY],
        out_shape=[
            jax.ShapeDtypeStruct(shape, F32),
            jax.ShapeDtypeStruct(PAIR, F32),
            jax.ShapeDtypeStruct(token.shape, F32),
        ],
        input_output_aliases=aliases,
        compiler_params=pltpu.CompilerParams(vmem_limit_bytes=40 * 1024 * 1024),
        cost_estimate=pl.CostEstimate(flops=int(weight * 1_000_000_000), bytes_accessed=tiles * 400_000, transcendentals=0),
        name=name,
    )(x, amps, q, tables, grad, *more)


def finish_kernel(a_ref, b_ref, ta_re, ta_im, tb_re, tb_im, mix, factor_ref, out_ref):
    a = product_conj(a_ref[0], a_ref[1], ta_re[...], ta_im[...])
    b = product_conj(b_ref[0], b_ref[1], tb_re[...], tb_im[...])
    for part in (0, 1):
        x = (a[part] + b[part]) * factor_ref[0]
        x = sum(dot(mix[1], piece) for piece in pieces(x))
        x = sum(dot(piece, mix[0]) for piece in pieces(x))
        out_ref[part, 0] = x[:, :HALF]
        out_ref[part, 1] = x[:, HALF:]


def pieces(x):
    high = x.astype(BF16)
    x = x - high.astype(F32)
    middle = x.astype(BF16)
    return high, middle, (x - middle.astype(F32)).astype(BF16)


def finished(grad_a, grad_b, turn_a, turn_b, mix, factor):
    vmem = pl.BlockSpec(memory_space=pltpu.VMEM)
    both = jnp.asarray(np.stack([mix, mix.T]).astype(BF16))
    return pl.pallas_call(
        finish_kernel,
        in_specs=[vmem] * 7 + [pl.BlockSpec(memory_space=pltpu.SMEM)],
        out_specs=vmem,
        out_shape=jax.ShapeDtypeStruct((2, 2, WIDTH, HALF), F32),
        compiler_params=pltpu.CompilerParams(vmem_limit_bytes=40 * 1024 * 1024),
        name="finish",
    )(grad_a, grad_b, *turn_a, *turn_b, both, jnp.full((1,), factor, F32))


def summed(parts):
    members = lax.axis_size("tile") * lax.axis_size("plane")
    mine = parts.reshape(members, -1, HALF)
    mine = lax.all_to_all(mine, AXES, 0, 0, tiled=True).sum(0)
    mine = jnp.broadcast_to(mine[None], (members, *mine.shape))
    total = lax.all_to_all(mine, AXES, 0, 0, tiled=True).reshape(2, 2, WIDTH, HALF)
    return total.transpose(0, 2, 1, 3).reshape(2, WIDTH, WIDTH)


def turned(distance):
    angle = distance * jnp.asarray(transfer_phase())
    return jnp.cos(angle), jnp.sin(angle)


def body(ring, fields, amplitudes, pupil, distances):
    planes, tiles_all = lax.axis_size("plane"), lax.axis_size("tile")
    fields, amps = fields[:, 0], amplitudes[0]
    count = amps.shape[0]
    factor = 1.0 / math.sqrt(STEPS * planes * tiles_all * count)
    tables = jnp.asarray(dft_tables())
    mix = shuffle()

    def sent(value, pairs):
        return lax.ppermute(value, "plane", pairs)

    ahead, behind = plane_pairs(1, planes), plane_pairs(-1, planes)
    back, rest = back_pairs(planes, ring), rest_pairs(planes, ring)

    amps_45 = sent(amps[4:6], behind)
    fields_01 = sent(fields[:, 0:2], ahead)
    distance_before = sent(distances, ahead)
    shuffled = jnp.einsum("ij,cjk,lk->cil", mix, pupil, mix, precision=lax.Precision.HIGHEST)
    turn_before, turn_here = turned(distance_before[0]), turned(distances[0])
    q_before = jnp.stack(product(shuffled[0], shuffled[1], *turn_before))
    q_here = jnp.stack(product(shuffled[0], shuffled[1], *turn_here))
    later_amps, later_fields, q_before = lax.optimization_barrier((amps, fields, q_before))
    amps_67 = sent(later_amps[6:8], behind)
    fields_23 = sent(later_fields[:, 2:4], ahead)

    grads = {"before": jnp.zeros(PAIR, F32), "here": jnp.zeros(PAIR, F32)}
    filters = {"before": q_before, "here": q_here}
    token = jnp.zeros((8, 128), F32)

    def first(which, x, x_at, a, a_at, tiles, weight, after=()):
        nonlocal token
        result, grads[which], token = step_call(
            first_kernel, x, x_at, a, a_at, filters[which], tables, grads[which], token, tiles, None, 0, tiles, after, weight, "first_step")
        return result

    out = None

    def second(x, at, tiles, weight):
        nonlocal token, out
        out, grads["before"], token = step_call(
            second_kernel, x, 0, amps, at, filters["before"], tables, grads["before"], token, tiles, out, at, count, (), weight, "second_step")

    weights = [30, 3, 30, 3, 0.1, 5, 0.1, 1]
    s_45 = sent(first("here", fields, 4, amps_45, 0, 2, weights[0]), back)
    s_6 = sent(first("here", fields, 6, amps_67, 0, 1, weights[1]), back)
    s_01 = sent(first("before", fields_01, 0, amps, 0, 2, weights[2]), ahead)
    s_7 = sent(first("here", fields, 7, amps_67, 1, 1, weights[3]), plane_pairs(2, planes))
    s_2 = sent(first("before", fields_23, 0, amps, 2, 1, weights[4]), ahead)
    s_3 = sent(first("before", fields_23, 1, amps, 3, 1, weights[5]), ahead)
    s_45 = sent(s_45, rest)
    s_6 = sent(s_6, rest)
    second(s_01, 0, 2, weights[6])
    second(s_7, 7, 1, weights[6])
    second(s_45, 4, 2, weights[6])
    second(s_2, 2, 1, weights[7])
    second(s_6, 6, 1, weights[7])
    second(s_3, 3, 1, weights[7])

    parts = finished(grads["before"], grads["here"], turn_before, turn_here, mix, 2.0 * factor)
    return (out[:, None], summed(parts))


def solution(mesh):
    placed = (P(None, "plane", "tile", None, None), P("plane", "tile", None, None), P(), P("plane"))
    ring = mesh.shape["plane"] // 2

    def step(*args):
        return body(ring, *args)

    return jax.shard_map(
        step,
        mesh=mesh,
        in_specs=placed,
        out_specs=(P(None, "plane", "tile", None, None), P()),
        check_vma=False,
    )
```

```python
import math

import jax
import jax.numpy as jnp
import numpy as np
from jax import lax
from jax.experimental import pallas as pl
from jax.experimental.pallas import tpu as pltpu
from jax.sharding import PartitionSpec as P

STEPS = 2
WIDTH = 256
HALF = WIDTH // 2
AXES = ("tile", "plane")
F32, BF16 = jnp.float32, jnp.bfloat16


def plane_pairs(steps, count):
    return [(source, (source + steps) % count) for source in range(count)]


def back_place(p, count, ring):
    return (p + 2) % count // ring * ring + (p % ring + ring - 1) % ring


def back_pairs(count, ring):
    return [(p, back_place(p, count, ring)) for p in range(count)]


def rest_pairs(count, ring):
    return [(back_place(p, count, ring), (p + 2) % count) for p in range(count)]


def order():
    return np.concatenate([np.arange(0, WIDTH, 2), np.arange(1, WIDTH, 2)])


def dft_halves():
    j, k = np.arange(HALF)[:, None], np.arange(HALF)[None, :]
    halves = []
    for odd in (0, 1):
        angle = -2.0 * np.pi * (j * (2 * k + odd) % WIDTH) / WIDTH
        re, im = np.cos(angle) / math.sqrt(WIDTH), np.sin(angle) / math.sqrt(WIDTH)
        halves.append(np.block([[re, im], [-im, re]]))
    return np.stack(halves)


def dft_tables():
    plain = dft_halves()
    full = np.concatenate([plain, plain.transpose(0, 2, 1)])
    high = full.astype(BF16)
    low = (full - high.astype(np.float64)).astype(BF16)
    return np.stack([high, low])


def transfer_phase():
    index = np.arange(WIDTH)
    freq = (((index + HALF) % WIDTH - HALF) / WIDTH)[order()]
    return (np.pi * (freq[:, None] ** 2 + freq[None, :] ** 2)).astype(np.float32)


def shuffle():
    return np.eye(WIDTH, dtype=np.float32)[order()]


def split(x):
    high = x.astype(BF16)
    return high, (x - high.astype(F32)).astype(BF16)


def dot(a, b):
    return jnp.dot(a, b, preferred_element_type=F32)


def right(t, tables, k):
    high, low = split(t)
    return dot(high, tables[0, k]) + (dot(low, tables[0, k]) + dot(high, tables[1, k]))


def left(tables, k, t):
    high, low = split(t)
    return dot(tables[0, k], high) + (dot(tables[0, k], low) + dot(tables[1, k], high))


def forward(re, im, tables):
    a = [re[:, :HALF], im[:, :HALF]]
    b = [re[:, HALF:], im[:, HALF:]]
    even = right(jnp.concatenate([a[0] + b[0], a[1] + b[1]], 1), tables, 0)
    odd = right(jnp.concatenate([a[0] - b[0], a[1] - b[1]], 1), tables, 1)
    re = jnp.concatenate([even[:, :HALF], odd[:, :HALF]], 1)
    im = jnp.concatenate([even[:, HALF:], odd[:, HALF:]], 1)
    a = [re[:HALF], im[:HALF]]
    b = [re[HALF:], im[HALF:]]
    even = left(tables, 2, jnp.concatenate([a[0] + b[0], a[1] + b[1]], 0))
    odd = left(tables, 3, jnp.concatenate([a[0] - b[0], a[1] - b[1]], 0))
    return (jnp.concatenate([even[:HALF], odd[:HALF]], 0), jnp.concatenate([even[HALF:], odd[HALF:]], 0))


def inverse(re, im, tables):
    even = left(tables, 0, jnp.concatenate([re[:HALF], im[:HALF]], 0))
    odd = left(tables, 1, jnp.concatenate([re[HALF:], im[HALF:]], 0))
    up, down = even + odd, even - odd
    re = jnp.concatenate([up[:HALF], down[:HALF]], 0)
    im = jnp.concatenate([up[HALF:], down[HALF:]], 0)
    even = right(jnp.concatenate([re[:, :HALF], im[:, :HALF]], 1), tables, 2)
    odd = right(jnp.concatenate([re[:, HALF:], im[:, HALF:]], 1), tables, 3)
    up, down = even + odd, even - odd
    return (
        jnp.concatenate([up[:, :HALF], down[:, :HALF]], 1),
        jnp.concatenate([up[:, HALF:], down[:, HALF:]], 1),
    )


def product(a_re, a_im, b_re, b_im):
    return a_re * b_re - a_im * b_im, a_re * b_im + a_im * b_re


def product_conj(a_re, a_im, b_re, b_im):
    return a_re * b_re + a_im * b_im, a_im * b_re - a_re * b_im


def constrained(u_re, u_im, amps):
    scale = amps * lax.rsqrt(u_re * u_re + u_im * u_im + 0.25)
    return u_re * scale, u_im * scale


def first_kernel(f_ref, a_ref, q_ref, tables, g_ref, *rest):
    spec_ref, grad_ref = rest[-3:-1]
    s_re, s_im = forward(f_ref[0, 0], f_ref[1, 0], tables)
    p_re, p_im = product(s_re, s_im, q_ref[0], q_ref[1])
    n_re, n_im = constrained(*inverse(p_re, p_im, tables), a_ref[0])
    n_re, n_im = forward(n_re, n_im, tables)
    spec_ref[0, 0] = n_re
    spec_ref[1, 0] = n_im
    add(g_ref, grad_ref, *product_conj(p_re - n_re, p_im - n_im, s_re, s_im))


def second_kernel(s_ref, a_ref, q_ref, tables, g_ref, *rest):
    out_ref, grad_ref = rest[-3:-1]
    s_re, s_im = s_ref[0, 0], s_ref[1, 0]
    u_re, u_im = inverse(*product(s_re, s_im, q_ref[0], q_ref[1]), tables)
    n_re, n_im = constrained(u_re, u_im, a_ref[0])
    out_ref[0, 0] = n_re
    out_ref[1, 0] = n_im
    w_re, w_im = forward(u_re - n_re, u_im - n_im, tables)
    add(g_ref, grad_ref, *product_conj(w_re, w_im, s_re, s_im))


def add(g_ref, grad_ref, g_re, g_im):
    @pl.when(pl.program_id(0) == 0)
    def _():
        grad_ref[...] = g_ref[...]

    grad_ref[0] += g_re
    grad_ref[1] += g_im


def tile_spec(shape, at):
    if len(shape) == 4:
        return pl.BlockSpec((2, 1, WIDTH, WIDTH), lambda i: (0, at + i, 0, 0))
    return pl.BlockSpec((1, WIDTH, WIDTH), lambda i: (at + i, 0, 0))


def whole(shape):
    return pl.BlockSpec(shape, lambda i: (0,) * len(shape))


ANY = pl.BlockSpec(memory_space=pl.ANY)
PAIR = (2, WIDTH, WIDTH)


def step_call(kernel, x, x_at, amps, a_at, q, tables, grad, token, tiles, out, out_at, out_tiles, after, weight, name):
    shape = (2, out_tiles, WIDTH, WIDTH)
    more = [token, *([] if out is None else [out]), *after]
    aliases = {4: 1, 5: 2} if out is None else {4: 1, 5: 2, 6: 0}
    return pl.pallas_call(
        kernel,
        grid=(tiles,),
        in_specs=[tile_spec(x.shape, x_at), tile_spec(amps.shape, a_at), whole(PAIR), whole(tables.shape), whole(PAIR)]
        + [ANY for _ in more],
        out_specs=[tile_spec(shape, out_at), whole(PAIR), ANY],
        out_shape=[
            jax.ShapeDtypeStruct(shape, F32),
            jax.ShapeDtypeStruct(PAIR, F32),
            jax.ShapeDtypeStruct(token.shape, F32),
        ],
        input_output_aliases=aliases,
        compiler_params=pltpu.CompilerParams(vmem_limit_bytes=40 * 1024 * 1024),
        cost_estimate=pl.CostEstimate(flops=int(weight * 1_000_000_000), bytes_accessed=tiles * 400_000, transcendentals=0),
        name=name,
    )(x, amps, q, tables, grad, *more)


def finish_kernel(a_ref, b_ref, ta_re, ta_im, tb_re, tb_im, mix, factor_ref, core_ref, mine_ref, others_ref):
    a = product_conj(a_ref[0], a_ref[1], ta_re[...], ta_im[...])
    b = product_conj(b_ref[0], b_ref[1], tb_re[...], tb_im[...])
    parts = []
    for part in (0, 1):
        x = (a[part] + b[part]) * factor_ref[0]
        x = sum(dot(mix[1], piece) for piece in pieces(x))
        parts.append(sum(dot(piece, mix[0]) for piece in pieces(x)))
    first_core = core_ref[0] == 0
    for ref, x in ((mine_ref, jnp.where(first_core, *parts)), (others_ref, jnp.where(first_core, *parts[::-1]))):
        ref[0] = x[:, :HALF]
        ref[1] = x[:, HALF:]


def pieces(x):
    high = x.astype(BF16)
    x = x - high.astype(F32)
    middle = x.astype(BF16)
    return high, middle, (x - middle.astype(F32)).astype(BF16)


def finished(grad_a, grad_b, turn_a, turn_b, mix, factor, core):
    vmem, smem = pl.BlockSpec(memory_space=pltpu.VMEM), pl.BlockSpec(memory_space=pltpu.SMEM)
    both = jnp.asarray(np.stack([mix, mix.T]).astype(BF16))
    part = jax.ShapeDtypeStruct((2, WIDTH, HALF), F32)
    return pl.pallas_call(
        finish_kernel,
        in_specs=[vmem] * 7 + [smem] * 2,
        out_specs=[vmem] * 2,
        out_shape=[part] * 2,
        compiler_params=pltpu.CompilerParams(vmem_limit_bytes=40 * 1024 * 1024),
        name="finish",
    )(grad_a, grad_b, *turn_a, *turn_b, both, jnp.full((1,), factor, F32), jnp.full((1,), core, jnp.int32))


def summed(mine, others, core):
    tiles, planes = lax.axis_size("tile"), lax.axis_size("plane")
    groups = [[t * planes + p for t in range(c, tiles, 2) for p in range(planes)] for c in (0, 1)]
    members = len(groups[0])
    swap = [(t * planes + p, (t ^ 1) * planes + p) for t in range(tiles) for p in range(planes)]
    mine = (mine + lax.ppermute(others, AXES, swap)).reshape(members, -1, HALF)
    mine = lax.all_to_all(mine, AXES, 0, 0, tiled=True, axis_index_groups=groups).sum(0)
    mine = jnp.broadcast_to(mine[None], (members, *mine.shape))
    mine = lax.all_to_all(mine, AXES, 0, 0, tiled=True, axis_index_groups=groups).reshape(2, WIDTH, HALF)
    others = lax.ppermute(mine, AXES, swap)
    total = jnp.where(core == 0, jnp.stack([mine, others]), jnp.stack([others, mine]))
    return total.transpose(0, 2, 1, 3).reshape(2, WIDTH, WIDTH)


def turned(distance):
    angle = distance * jnp.asarray(transfer_phase())
    return jnp.cos(angle), jnp.sin(angle)


def body(ring, fields, amplitudes, pupil, distances):
    planes, tiles_all = lax.axis_size("plane"), lax.axis_size("tile")
    fields, amps = fields[:, 0], amplitudes[0]
    count = amps.shape[0]
    factor = 1.0 / math.sqrt(STEPS * planes * tiles_all * count)
    tables = jnp.asarray(dft_tables())
    mix = shuffle()

    def sent(value, pairs):
        return lax.ppermute(value, "plane", pairs)

    ahead, behind = plane_pairs(1, planes), plane_pairs(-1, planes)
    back, rest = back_pairs(planes, ring), rest_pairs(planes, ring)

    amps_45 = sent(amps[4:6], behind)
    fields_01 = sent(fields[:, 0:2], ahead)
    distance_before = sent(distances, ahead)
    shuffled = jnp.einsum("ij,cjk,lk->cil", mix, pupil, mix, precision=lax.Precision.HIGHEST)
    turn_before, turn_here = turned(distance_before[0]), turned(distances[0])
    q_before = jnp.stack(product(shuffled[0], shuffled[1], *turn_before))
    q_here = jnp.stack(product(shuffled[0], shuffled[1], *turn_here))
    later_amps, later_fields, q_before = lax.optimization_barrier((amps, fields, q_before))
    amps_67 = sent(later_amps[6:8], behind)
    fields_23 = sent(later_fields[:, 2:4], ahead)

    grads = {"before": jnp.zeros(PAIR, F32), "here": jnp.zeros(PAIR, F32)}
    filters = {"before": q_before, "here": q_here}
    token = jnp.zeros((8, 128), F32)

    def first(which, x, x_at, a, a_at, tiles, weight, after=()):
        nonlocal token
        result, grads[which], token = step_call(
            first_kernel, x, x_at, a, a_at, filters[which], tables, grads[which], token, tiles, None, 0, tiles, after, weight, "first_step")
        return result

    out = None

    def second(x, at, tiles, weight):
        nonlocal token, out
        out, grads["before"], token = step_call(
            second_kernel, x, 0, amps, at, filters["before"], tables, grads["before"], token, tiles, out, at, count, (), weight, "second_step")

    weights = [30, 3, 30, 3, 0.1, 5, 0.1, 1]
    s_45 = sent(first("here", fields, 4, amps_45, 0, 2, weights[0]), back)
    s_6 = sent(first("here", fields, 6, amps_67, 0, 1, weights[1]), back)
    s_01 = sent(first("before", fields_01, 0, amps, 0, 2, weights[2]), ahead)
    s_7 = sent(first("here", fields, 7, amps_67, 1, 1, weights[3]), plane_pairs(2, planes))
    s_2 = sent(first("before", fields_23, 0, amps, 2, 1, weights[4]), ahead)
    s_3 = sent(first("before", fields_23, 1, amps, 3, 1, weights[5]), ahead)
    s_45 = sent(s_45, rest)
    s_6 = sent(s_6, rest)
    second(s_01, 0, 2, weights[6])
    second(s_7, 7, 1, weights[6])
    second(s_45, 4, 2, weights[6])
    second(s_2, 2, 1, weights[7])
    second(s_6, 6, 1, weights[7])
    second(s_3, 3, 1, weights[7])

    core = lax.axis_index("tile") % 2
    mine, others = finished(grads["before"], grads["here"], turn_before, turn_here, mix, 2.0 * factor, core)
    return (out[:, None], summed(mine, others, core))


def solution(mesh):
    placed = (P(None, "plane", "tile", None, None), P("plane", "tile", None, None), P(), P("plane"))
    ring = mesh.shape["plane"] // 2

    def step(*args):
        return body(ring, *args)

    return jax.shard_map(
        step,
        mesh=mesh,
        in_specs=placed,
        out_specs=(P(None, "plane", "tile", None, None), P()),
        check_vma=False,
    )
```

```python
import math

import jax
import jax.numpy as jnp
import numpy as np
from jax import lax
from jax.experimental import pallas as pl
from jax.experimental.pallas import tpu as pltpu
from jax.sharding import PartitionSpec as P

STEPS = 2
WIDTH = 256
HALF = WIDTH // 2
AXES = ("tile", "plane")
F32, BF16 = jnp.float32, jnp.bfloat16


def plane_pairs(steps, count):
    return [(source, (source + steps) % count) for source in range(count)]


def back_place(p, count, ring):
    return (p + 2) % count // ring * ring + (p % ring + ring - 1) % ring


def back_pairs(count, ring):
    return [(p, back_place(p, count, ring)) for p in range(count)]


def rest_pairs(count, ring):
    return [(back_place(p, count, ring), (p + 2) % count) for p in range(count)]


def order():
    return np.concatenate([np.arange(0, WIDTH, 2), np.arange(1, WIDTH, 2)])


def dft_halves():
    j, k = np.arange(HALF)[:, None], np.arange(HALF)[None, :]
    halves = []
    for odd in (0, 1):
        angle = -2.0 * np.pi * (j * (2 * k + odd) % WIDTH) / WIDTH
        re, im = np.cos(angle) / math.sqrt(WIDTH), np.sin(angle) / math.sqrt(WIDTH)
        halves.append(np.block([[re, im], [-im, re]]))
    return np.stack(halves)


def dft_tables():
    plain = dft_halves()
    full = np.concatenate([plain, plain.transpose(0, 2, 1)])
    high = full.astype(BF16)
    low = (full - high.astype(np.float64)).astype(BF16)
    return np.stack([high, low])


def transfer_phase():
    index = np.arange(WIDTH)
    freq = (((index + HALF) % WIDTH - HALF) / WIDTH)[order()]
    return (np.pi * (freq[:, None] ** 2 + freq[None, :] ** 2)).astype(np.float32)


def shuffle():
    return np.eye(WIDTH, dtype=np.float32)[order()]


def split(x):
    high = x.astype(BF16)
    return high, (x - high.astype(F32)).astype(BF16)


def dot(a, b):
    return jnp.dot(a, b, preferred_element_type=F32)


def right(t, tables, k):
    high, low = split(t)
    return dot(high, tables[0, k]) + (dot(low, tables[0, k]) + dot(high, tables[1, k]))


def left(tables, k, t):
    high, low = split(t)
    return dot(tables[0, k], high) + (dot(tables[0, k], low) + dot(tables[1, k], high))


def forward(re, im, tables):
    a = [re[:, :HALF], im[:, :HALF]]
    b = [re[:, HALF:], im[:, HALF:]]
    even = right(jnp.concatenate([a[0] + b[0], a[1] + b[1]], 1), tables, 0)
    odd = right(jnp.concatenate([a[0] - b[0], a[1] - b[1]], 1), tables, 1)
    re = jnp.concatenate([even[:, :HALF], odd[:, :HALF]], 1)
    im = jnp.concatenate([even[:, HALF:], odd[:, HALF:]], 1)
    a = [re[:HALF], im[:HALF]]
    b = [re[HALF:], im[HALF:]]
    even = left(tables, 2, jnp.concatenate([a[0] + b[0], a[1] + b[1]], 0))
    odd = left(tables, 3, jnp.concatenate([a[0] - b[0], a[1] - b[1]], 0))
    return (jnp.concatenate([even[:HALF], odd[:HALF]], 0), jnp.concatenate([even[HALF:], odd[HALF:]], 0))


def inverse(re, im, tables):
    even = left(tables, 0, jnp.concatenate([re[:HALF], im[:HALF]], 0))
    odd = left(tables, 1, jnp.concatenate([re[HALF:], im[HALF:]], 0))
    up, down = even + odd, even - odd
    re = jnp.concatenate([up[:HALF], down[:HALF]], 0)
    im = jnp.concatenate([up[HALF:], down[HALF:]], 0)
    even = right(jnp.concatenate([re[:, :HALF], im[:, :HALF]], 1), tables, 2)
    odd = right(jnp.concatenate([re[:, HALF:], im[:, HALF:]], 1), tables, 3)
    up, down = even + odd, even - odd
    return (
        jnp.concatenate([up[:, :HALF], down[:, :HALF]], 1),
        jnp.concatenate([up[:, HALF:], down[:, HALF:]], 1),
    )


def product(a_re, a_im, b_re, b_im):
    return a_re * b_re - a_im * b_im, a_re * b_im + a_im * b_re


def product_conj(a_re, a_im, b_re, b_im):
    return a_re * b_re + a_im * b_im, a_im * b_re - a_re * b_im


def constrained(u_re, u_im, amps):
    scale = amps * lax.rsqrt(u_re * u_re + u_im * u_im + 0.25)
    return u_re * scale, u_im * scale


def first_kernel(f_ref, a_ref, q_ref, tables, g_ref, *rest):
    spec_ref, grad_ref = rest[-3:-1]
    s_re, s_im = forward(f_ref[0, 0], f_ref[1, 0], tables)
    p_re, p_im = product(s_re, s_im, q_ref[0], q_ref[1])
    n_re, n_im = constrained(*inverse(p_re, p_im, tables), a_ref[0])
    n_re, n_im = forward(n_re, n_im, tables)
    spec_ref[0, 0] = n_re
    spec_ref[1, 0] = n_im
    add(g_ref, grad_ref, *product_conj(p_re - n_re, p_im - n_im, s_re, s_im))


def second_kernel(s_ref, a_ref, q_ref, tables, g_ref, *rest):
    out_ref, grad_ref = rest[-3:-1]
    s_re, s_im = s_ref[0, 0], s_ref[1, 0]
    u_re, u_im = inverse(*product(s_re, s_im, q_ref[0], q_ref[1]), tables)
    n_re, n_im = constrained(u_re, u_im, a_ref[0])
    out_ref[0, 0] = n_re
    out_ref[1, 0] = n_im
    w_re, w_im = forward(u_re - n_re, u_im - n_im, tables)
    add(g_ref, grad_ref, *product_conj(w_re, w_im, s_re, s_im))


def last_kernel(s_ref, a_ref, q_ref, tables, g_ref, other_ref, *rest):
    first_one = pl.program_id(0) == 0

    class Chosen:
        def __getitem__(self, at):
            return jnp.where(first_one, s_ref[at], other_ref[at])

    second_kernel(Chosen(), a_ref, q_ref, tables, g_ref, *rest)


def add(g_ref, grad_ref, g_re, g_im):
    @pl.when(pl.program_id(0) == 0)
    def _():
        grad_ref[...] = g_ref[...]

    grad_ref[0] += g_re
    grad_ref[1] += g_im


def tile_spec(shape, at, stride=1):
    if len(shape) == 4:
        return pl.BlockSpec((2, 1, WIDTH, WIDTH), lambda i: (0, at + i * stride, 0, 0))
    return pl.BlockSpec((1, WIDTH, WIDTH), lambda i: (at + i * stride, 0, 0))


def whole(shape):
    return pl.BlockSpec(shape, lambda i: (0,) * len(shape))


ANY = pl.BlockSpec(memory_space=pl.ANY)
PAIR = (2, WIDTH, WIDTH)


def step_call(kernel, x, x_at, amps, a_at, q, tables, grad, token, tiles, out, out_at, out_tiles, after, weight, name):
    shape = (2, out_tiles, WIDTH, WIDTH)
    more = [token, *([] if out is None else [out]), *after]
    aliases = {4: 1, 5: 2} if out is None else {4: 1, 5: 2, 6: 0}
    return pl.pallas_call(
        kernel,
        grid=(tiles,),
        in_specs=[tile_spec(x.shape, x_at), tile_spec(amps.shape, a_at), whole(PAIR), whole(tables.shape), whole(PAIR)]
        + [ANY for _ in more],
        out_specs=[tile_spec(shape, out_at), whole(PAIR), ANY],
        out_shape=[
            jax.ShapeDtypeStruct(shape, F32),
            jax.ShapeDtypeStruct(PAIR, F32),
            jax.ShapeDtypeStruct(token.shape, F32),
        ],
        input_output_aliases=aliases,
        compiler_params=pltpu.CompilerParams(vmem_limit_bytes=40 * 1024 * 1024),
        cost_estimate=pl.CostEstimate(flops=int(weight * 1_000_000_000), bytes_accessed=tiles * 400_000, transcendentals=0),
        name=name,
    )(x, amps, q, tables, grad, *more)


def last_step(x, other, amps, at, other_at, q, tables, grad, token, out):
    stride = other_at - at
    return pl.pallas_call(
        last_kernel,
        grid=(2,),
        in_specs=[whole(x.shape), tile_spec(amps.shape, at, stride), whole(PAIR), whole(tables.shape), whole(PAIR)]
        + [whole(other.shape), ANY, ANY],
        out_specs=[tile_spec(out.shape, at, stride), whole(PAIR), ANY],
        out_shape=[jax.ShapeDtypeStruct(y.shape, F32) for y in (out, grad, token)],
        input_output_aliases={4: 1, 6: 2, 7: 0},
        compiler_params=pltpu.CompilerParams(vmem_limit_bytes=40 * 1024 * 1024),
        cost_estimate=pl.CostEstimate(flops=1_000_000_000, bytes_accessed=800_000, transcendentals=0),
        name="second_step",
    )(x, amps, q, tables, grad, other, token, out)


def laid_out(parts):
    def kernel(in_ref, out_ref):
        out_ref[0, :, :HALF] = in_ref[0, 0]
        out_ref[0, :, HALF:] = in_ref[0, 1]

    return pl.pallas_call(
        kernel,
        grid=(2,),
        in_specs=[pl.BlockSpec((1, 2, WIDTH, HALF), lambda i: (i, 0, 0, 0))],
        out_specs=pl.BlockSpec((1, WIDTH, WIDTH), lambda i: (i, 0, 0)),
        out_shape=jax.ShapeDtypeStruct(PAIR, F32),
        name="laid_out",
    )(parts)


def finish_kernel(a_ref, b_ref, ta_re, ta_im, tb_re, tb_im, mix, factor_ref, out_ref):
    a = product_conj(a_ref[0], a_ref[1], ta_re[...], ta_im[...])
    b = product_conj(b_ref[0], b_ref[1], tb_re[...], tb_im[...])
    for part in (0, 1):
        x = (a[part] + b[part]) * factor_ref[0]
        x = sum(dot(mix[1], piece) for piece in pieces(x))
        x = sum(dot(piece, mix[0]) for piece in pieces(x))
        out_ref[part, 0] = x[:, :HALF]
        out_ref[part, 1] = x[:, HALF:]


def pieces(x):
    high = x.astype(BF16)
    x = x - high.astype(F32)
    middle = x.astype(BF16)
    return high, middle, (x - middle.astype(F32)).astype(BF16)


def finished(grad_a, grad_b, turn_a, turn_b, mix, factor):
    vmem = pl.BlockSpec(memory_space=pltpu.VMEM)
    both = jnp.asarray(np.stack([mix, mix.T]).astype(BF16))
    return pl.pallas_call(
        finish_kernel,
        in_specs=[vmem] * 7 + [pl.BlockSpec(memory_space=pltpu.SMEM)],
        out_specs=vmem,
        out_shape=jax.ShapeDtypeStruct((2, 2, WIDTH, HALF), F32),
        compiler_params=pltpu.CompilerParams(vmem_limit_bytes=40 * 1024 * 1024),
        name="finish",
    )(grad_a, grad_b, *turn_a, *turn_b, both, jnp.full((1,), factor, F32))


def summed(parts):
    members = lax.axis_size("tile") * lax.axis_size("plane")
    mine = parts.reshape(members, -1, HALF)
    mine = lax.all_to_all(mine, AXES, 0, 0, tiled=True).sum(0)
    mine = jnp.broadcast_to(mine[None], (members, *mine.shape))
    total = lax.all_to_all(mine, AXES, 0, 0, tiled=True).reshape(2, 2, WIDTH, HALF)
    return laid_out(total)


def turned(distance):
    angle = distance * jnp.asarray(transfer_phase())
    return jnp.cos(angle), jnp.sin(angle)


def body(ring, fields, amplitudes, pupil, distances):
    planes, tiles_all = lax.axis_size("plane"), lax.axis_size("tile")
    fields, amps = fields[:, 0], amplitudes[0]
    count = amps.shape[0]
    factor = 1.0 / math.sqrt(STEPS * planes * tiles_all * count)
    tables = jnp.asarray(dft_tables())
    mix = shuffle()

    def sent(value, pairs):
        return lax.ppermute(value, "plane", pairs)

    ahead, behind = plane_pairs(1, planes), plane_pairs(-1, planes)
    back, rest = back_pairs(planes, ring), rest_pairs(planes, ring)

    amps_45 = sent(amps[4:6], behind)
    fields_01 = sent(fields[:, 0:2], ahead)
    distance_before = sent(distances, ahead)
    shuffled = jnp.einsum("ij,cjk,lk->cil", mix, pupil, mix, precision=lax.Precision.HIGHEST)
    turn_before, turn_here = turned(distance_before[0]), turned(distances[0])
    q_before = jnp.stack(product(shuffled[0], shuffled[1], *turn_before))
    q_here = jnp.stack(product(shuffled[0], shuffled[1], *turn_here))
    later_amps, later_fields, q_before = lax.optimization_barrier((amps, fields, q_before))
    amps_67 = sent(later_amps[6:8], behind)
    fields_23 = sent(later_fields[:, 2:4], ahead)

    grads = {"before": jnp.zeros(PAIR, F32), "here": jnp.zeros(PAIR, F32)}
    filters = {"before": q_before, "here": q_here}
    token = jnp.zeros((8, 128), F32)

    def first(which, x, x_at, a, a_at, tiles, weight, after=()):
        nonlocal token
        result, grads[which], token = step_call(
            first_kernel, x, x_at, a, a_at, filters[which], tables, grads[which], token, tiles, None, 0, tiles, after, weight, "first_step")
        return result

    out = None

    def second(x, at, tiles, weight):
        nonlocal token, out
        out, grads["before"], token = step_call(
            second_kernel, x, 0, amps, at, filters["before"], tables, grads["before"], token, tiles, out, at, count, (), weight, "second_step")

    weights = [30, 3, 30, 3, 0.1, 5, 0.1, 1]
    s_45 = sent(first("here", fields, 4, amps_45, 0, 2, weights[0]), back)
    s_6 = sent(first("here", fields, 6, amps_67, 0, 1, weights[1]), back)
    s_01 = sent(first("before", fields_01, 0, amps, 0, 2, weights[2]), ahead)
    s_7 = sent(first("here", fields, 7, amps_67, 1, 1, weights[3]), plane_pairs(2, planes))
    s_2 = sent(first("before", fields_23, 0, amps, 2, 1, weights[4]), ahead)
    s_3 = sent(first("before", fields_23, 1, amps, 3, 1, weights[5]), ahead)
    s_45 = sent(s_45, rest)
    s_6 = sent(s_6, rest)
    second(s_01, 0, 2, weights[6])
    second(s_7, 7, 1, weights[6])
    second(s_45, 4, 2, weights[6])
    second(s_2, 2, 1, weights[7])
    out, grads["before"], token = last_step(
        s_6, s_3, amps, 6, 3, filters["before"], tables, grads["before"], token, out)

    parts = finished(grads["before"], grads["here"], turn_before, turn_here, mix, 2.0 * factor)
    return (out[:, None], summed(parts))


def solution(mesh):
    placed = (P(None, "plane", "tile", None, None), P("plane", "tile", None, None), P(), P("plane"))
    ring = mesh.shape["plane"] // 2

    def step(*args):
        return body(ring, *args)

    return jax.shard_map(
        step,
        mesh=mesh,
        in_specs=placed,
        out_specs=(P(None, "plane", "tile", None, None), P()),
        check_vma=False,
    )
```

```python
import math

import jax
import jax.numpy as jnp
import numpy as np
from jax import lax
from jax.experimental import pallas as pl
from jax.experimental.pallas import tpu as pltpu
from jax.sharding import PartitionSpec as P

STEPS = 2
WIDTH = 256
HALF = WIDTH // 2
AXES = ("tile", "plane")
F32, BF16 = jnp.float32, jnp.bfloat16


def plane_pairs(steps, count):
    return [(source, (source + steps) % count) for source in range(count)]


def back_place(p, count, ring):
    return (p + 2) % count // ring * ring + (p % ring + ring - 1) % ring


def back_pairs(count, ring):
    return [(p, back_place(p, count, ring)) for p in range(count)]


def rest_pairs(count, ring):
    return [(back_place(p, count, ring), (p + 2) % count) for p in range(count)]


def order():
    return np.concatenate([np.arange(0, WIDTH, 2), np.arange(1, WIDTH, 2)])


def dft_halves():
    j, k = np.arange(HALF)[:, None], np.arange(HALF)[None, :]
    halves = []
    for odd in (0, 1):
        angle = -2.0 * np.pi * (j * (2 * k + odd) % WIDTH) / WIDTH
        re, im = np.cos(angle) / math.sqrt(WIDTH), np.sin(angle) / math.sqrt(WIDTH)
        halves.append(np.block([[re, im], [-im, re]]))
    return np.stack(halves)


def dft_tables():
    plain = dft_halves()
    full = np.concatenate([plain, plain.transpose(0, 2, 1)])
    high = full.astype(BF16)
    low = (full - high.astype(np.float64)).astype(BF16)
    return np.stack([high, low])


def transfer_phase():
    index = np.arange(WIDTH)
    freq = (((index + HALF) % WIDTH - HALF) / WIDTH)[order()]
    return (np.pi * (freq[:, None] ** 2 + freq[None, :] ** 2)).astype(np.float32)


def shuffle():
    return np.eye(WIDTH, dtype=np.float32)[order()]


def split(x):
    high = x.astype(BF16)
    return high, (x - high.astype(F32)).astype(BF16)


def dot(a, b):
    return jnp.dot(a, b, preferred_element_type=F32)


def right(t, tables, k):
    high, low = split(t)
    return dot(high, tables[0, k]) + (dot(low, tables[0, k]) + dot(high, tables[1, k]))


def left(tables, k, t):
    high, low = split(t)
    return dot(tables[0, k], high) + (dot(tables[0, k], low) + dot(tables[1, k], high))


def forward(re, im, tables):
    a = [re[:, :HALF], im[:, :HALF]]
    b = [re[:, HALF:], im[:, HALF:]]
    even = right(jnp.concatenate([a[0] + b[0], a[1] + b[1]], 1), tables, 0)
    odd = right(jnp.concatenate([a[0] - b[0], a[1] - b[1]], 1), tables, 1)
    re = jnp.concatenate([even[:, :HALF], odd[:, :HALF]], 1)
    im = jnp.concatenate([even[:, HALF:], odd[:, HALF:]], 1)
    a = [re[:HALF], im[:HALF]]
    b = [re[HALF:], im[HALF:]]
    even = left(tables, 2, jnp.concatenate([a[0] + b[0], a[1] + b[1]], 0))
    odd = left(tables, 3, jnp.concatenate([a[0] - b[0], a[1] - b[1]], 0))
    return (jnp.concatenate([even[:HALF], odd[:HALF]], 0), jnp.concatenate([even[HALF:], odd[HALF:]], 0))


def inverse(re, im, tables):
    even = left(tables, 0, jnp.concatenate([re[:HALF], im[:HALF]], 0))
    odd = left(tables, 1, jnp.concatenate([re[HALF:], im[HALF:]], 0))
    up, down = even + odd, even - odd
    re = jnp.concatenate([up[:HALF], down[:HALF]], 0)
    im = jnp.concatenate([up[HALF:], down[HALF:]], 0)
    even = right(jnp.concatenate([re[:, :HALF], im[:, :HALF]], 1), tables, 2)
    odd = right(jnp.concatenate([re[:, HALF:], im[:, HALF:]], 1), tables, 3)
    up, down = even + odd, even - odd
    return (
        jnp.concatenate([up[:, :HALF], down[:, :HALF]], 1),
        jnp.concatenate([up[:, HALF:], down[:, HALF:]], 1),
    )


def product(a_re, a_im, b_re, b_im):
    return a_re * b_re - a_im * b_im, a_re * b_im + a_im * b_re


def product_conj(a_re, a_im, b_re, b_im):
    return a_re * b_re + a_im * b_im, a_im * b_re - a_re * b_im


def constrained(u_re, u_im, amps):
    scale = amps * lax.rsqrt(u_re * u_re + u_im * u_im + 0.25)
    return u_re * scale, u_im * scale


def first_kernel(f_ref, a_ref, q_ref, tables, g_ref, *rest):
    spec_ref, grad_ref = rest[-3:-1]
    s_re, s_im = forward(f_ref[0, 0], f_ref[1, 0], tables)
    p_re, p_im = product(s_re, s_im, q_ref[0], q_ref[1])
    n_re, n_im = constrained(*inverse(p_re, p_im, tables), a_ref[0])
    n_re, n_im = forward(n_re, n_im, tables)
    spec_ref[0, 0] = n_re
    spec_ref[1, 0] = n_im
    add(g_ref, grad_ref, *product_conj(p_re - n_re, p_im - n_im, s_re, s_im))


def second_kernel(s_ref, a_ref, q_ref, tables, g_ref, *rest):
    out_ref, grad_ref = rest[-3:-1]
    s_re, s_im = s_ref[0, 0], s_ref[1, 0]
    u_re, u_im = inverse(*product(s_re, s_im, q_ref[0], q_ref[1]), tables)
    n_re, n_im = constrained(u_re, u_im, a_ref[0])
    out_ref[0, 0] = n_re
    out_ref[1, 0] = n_im
    w_re, w_im = forward(u_re - n_re, u_im - n_im, tables)
    add(g_ref, grad_ref, *product_conj(w_re, w_im, s_re, s_im))


def last_kernel(s_ref, a_ref, q_ref, tables, g_ref, other_ref, *rest):
    first_one = pl.program_id(0) == 0

    class Chosen:
        def __getitem__(self, at):
            return jnp.where(first_one, s_ref[at], other_ref[at])

    second_kernel(Chosen(), a_ref, q_ref, tables, g_ref, *rest)


def add(g_ref, grad_ref, g_re, g_im):
    @pl.when(pl.program_id(0) == 0)
    def _():
        grad_ref[...] = g_ref[...]

    grad_ref[0] += g_re
    grad_ref[1] += g_im


def tile_spec(shape, at, stride=1):
    if len(shape) == 4:
        return pl.BlockSpec((2, 1, WIDTH, WIDTH), lambda i: (0, at + i * stride, 0, 0))
    return pl.BlockSpec((1, WIDTH, WIDTH), lambda i: (at + i * stride, 0, 0))


def whole(shape):
    return pl.BlockSpec(shape, lambda i: (0,) * len(shape))


ANY = pl.BlockSpec(memory_space=pl.ANY)
PAIR = (2, WIDTH, WIDTH)


def step_call(kernel, x, x_at, amps, a_at, q, tables, grad, token, tiles, out, out_at, out_tiles, after, weight, name):
    shape = (2, out_tiles, WIDTH, WIDTH)
    more = [token, *([] if out is None else [out]), *after]
    aliases = {4: 1, 5: 2} if out is None else {4: 1, 5: 2, 6: 0}
    return pl.pallas_call(
        kernel,
        grid=(tiles,),
        in_specs=[tile_spec(x.shape, x_at), tile_spec(amps.shape, a_at), whole(PAIR), whole(tables.shape), whole(PAIR)]
        + [ANY for _ in more],
        out_specs=[tile_spec(shape, out_at), whole(PAIR), ANY],
        out_shape=[
            jax.ShapeDtypeStruct(shape, F32),
            jax.ShapeDtypeStruct(PAIR, F32),
            jax.ShapeDtypeStruct(token.shape, F32),
        ],
        input_output_aliases=aliases,
        compiler_params=pltpu.CompilerParams(vmem_limit_bytes=40 * 1024 * 1024),
        cost_estimate=pl.CostEstimate(flops=int(weight * 1_000_000_000), bytes_accessed=tiles * 400_000, transcendentals=0),
        name=name,
    )(x, amps, q, tables, grad, *more)


def last_step(x, other, amps, at, other_at, q, tables, grad, token, out):
    stride = other_at - at
    return pl.pallas_call(
        last_kernel,
        grid=(2,),
        in_specs=[whole(x.shape), tile_spec(amps.shape, at, stride), whole(PAIR), whole(tables.shape), whole(PAIR)]
        + [whole(other.shape), ANY, ANY],
        out_specs=[tile_spec(out.shape, at, stride), whole(PAIR), ANY],
        out_shape=[jax.ShapeDtypeStruct(y.shape, F32) for y in (out, grad, token)],
        input_output_aliases={4: 1, 6: 2, 7: 0},
        compiler_params=pltpu.CompilerParams(vmem_limit_bytes=40 * 1024 * 1024),
        cost_estimate=pl.CostEstimate(flops=1_000_000_000, bytes_accessed=800_000, transcendentals=0),
        name="second_step",
    )(x, amps, q, tables, grad, other, token, out)


def finish_kernel(a_ref, b_ref, ta_re, ta_im, tb_re, tb_im, mix, factor_ref, out_ref):
    a = product_conj(a_ref[0], a_ref[1], ta_re[...], ta_im[...])
    b = product_conj(b_ref[0], b_ref[1], tb_re[...], tb_im[...])
    for part in (0, 1):
        x = (a[part] + b[part]) * factor_ref[0]
        x = sum(dot(mix[1], piece) for piece in pieces(x))
        x = sum(dot(piece, mix[0]) for piece in pieces(x))
        out_ref[part, 0] = x[:, :HALF]
        out_ref[part, 1] = x[:, HALF:]


def pieces(x):
    high = x.astype(BF16)
    x = x - high.astype(F32)
    middle = x.astype(BF16)
    return high, middle, (x - middle.astype(F32)).astype(BF16)


def finished(grad_a, grad_b, turn_a, turn_b, mix, factor):
    vmem = pl.BlockSpec(memory_space=pltpu.VMEM)
    both = jnp.asarray(np.stack([mix, mix.T]).astype(BF16))
    return pl.pallas_call(
        finish_kernel,
        in_specs=[vmem] * 7 + [pl.BlockSpec(memory_space=pltpu.SMEM)],
        out_specs=vmem,
        out_shape=jax.ShapeDtypeStruct((2, 2, WIDTH, HALF), F32),
        compiler_params=pltpu.CompilerParams(vmem_limit_bytes=40 * 1024 * 1024),
        name="finish",
    )(grad_a, grad_b, *turn_a, *turn_b, both, jnp.full((1,), factor, F32))


def summed(parts):
    members = lax.axis_size("tile") * lax.axis_size("plane")
    mine = parts.reshape(members, -1, HALF)
    mine = lax.all_to_all(mine, AXES, 0, 0, tiled=True).sum(0)
    mine = jnp.broadcast_to(mine[None], (members, *mine.shape))
    total = lax.all_to_all(mine, AXES, 0, 0, tiled=True).reshape(2, 2, WIDTH, HALF)
    return total.transpose(0, 2, 1, 3).reshape(2, WIDTH, WIDTH)


def turned(distance):
    angle = distance * jnp.asarray(transfer_phase())
    return jnp.cos(angle), jnp.sin(angle)


def body(ring, fields, amplitudes, pupil, distances):
    planes, tiles_all = lax.axis_size("plane"), lax.axis_size("tile")
    fields, amps = fields[:, 0], amplitudes[0]
    count = amps.shape[0]
    factor = 1.0 / math.sqrt(STEPS * planes * tiles_all * count)
    tables = jnp.asarray(dft_tables())
    mix = shuffle()

    def sent(value, pairs):
        return lax.ppermute(value, "plane", pairs)

    ahead, behind = plane_pairs(1, planes), plane_pairs(-1, planes)
    back, rest = back_pairs(planes, ring), rest_pairs(planes, ring)

    amps_45 = sent(amps[4:6], behind)
    fields_01 = sent(fields[:, 0:2], ahead)
    distance_before = sent(distances, ahead)
    shuffled = jnp.einsum("ij,cjk,lk->cil", mix, pupil, mix, precision=lax.Precision.HIGHEST)
    turn_before, turn_here = turned(distance_before[0]), turned(distances[0])
    q_before = jnp.stack(product(shuffled[0], shuffled[1], *turn_before))
    q_here = jnp.stack(product(shuffled[0], shuffled[1], *turn_here))
    later_amps, later_fields, q_before = lax.optimization_barrier((amps, fields, q_before))
    amps_67 = sent(later_amps[6:8], behind)
    fields_23 = sent(later_fields[:, 2:4], ahead)

    grads = {"before": jnp.zeros(PAIR, F32), "here": jnp.zeros(PAIR, F32)}
    filters = {"before": q_before, "here": q_here}
    token = jnp.zeros((8, 128), F32)

    def first(which, x, x_at, a, a_at, tiles, weight, after=()):
        nonlocal token
        result, grads[which], token = step_call(
            first_kernel, x, x_at, a, a_at, filters[which], tables, grads[which], token, tiles, None, 0, tiles, after, weight, "first_step")
        return result

    out = None

    def second(x, at, tiles, weight):
        nonlocal token, out
        out, grads["before"], token = step_call(
            second_kernel, x, 0, amps, at, filters["before"], tables, grads["before"], token, tiles, out, at, count, (), weight, "second_step")

    weights = [5, 30, 3, 1, 0.1, 5, 3, 10]
    s_45 = sent(first("here", fields, 4, amps_45, 0, 2, weights[0]), back)
    s_6 = sent(first("here", fields, 6, amps_67, 0, 1, weights[1]), back)
    s_01 = sent(first("before", fields_01, 0, amps, 0, 2, weights[2]), ahead)
    s_7 = sent(first("here", fields, 7, amps_67, 1, 1, weights[3]), plane_pairs(2, planes))
    s_2 = sent(first("before", fields_23, 0, amps, 2, 1, weights[4]), ahead)
    s_3 = sent(first("before", fields_23, 1, amps, 3, 1, weights[5]), ahead)
    s_45 = sent(s_45, rest)
    s_6 = sent(s_6, rest)
    second(s_01, 0, 2, weights[6])
    second(s_7, 7, 1, weights[6])
    second(s_45, 4, 2, weights[6])
    second(s_2, 2, 1, weights[7])
    out, grads["before"], token = last_step(
        s_6, s_3, amps, 6, 3, filters["before"], tables, grads["before"], token, out)

    parts = finished(grads["before"], grads["here"], turn_before, turn_here, mix, 2.0 * factor)
    return (out[:, None], summed(parts))


def solution(mesh):
    placed = (P(None, "plane", "tile", None, None), P("plane", "tile", None, None), P(), P("plane"))
    ring = mesh.shape["plane"] // 2

    def step(*args):
        return body(ring, *args)

    return jax.shard_map(
        step,
        mesh=mesh,
        in_specs=placed,
        out_specs=(P(None, "plane", "tile", None, None), P()),
        check_vma=False,
    )
```

```python
import math

import jax
import jax.numpy as jnp
import numpy as np
from jax import lax
from jax.experimental import pallas as pl
from jax.experimental.pallas import tpu as pltpu
from jax.sharding import PartitionSpec as P

STEPS = 2
WIDTH = 256
HALF = WIDTH // 2
AXES = ("tile", "plane")
F32, BF16 = jnp.float32, jnp.bfloat16


def plane_pairs(steps, count):
    return [(source, (source + steps) % count) for source in range(count)]


def back_place(p, count, ring):
    return (p + 2) % count // ring * ring + (p % ring + ring - 1) % ring


def back_pairs(count, ring):
    return [(p, back_place(p, count, ring)) for p in range(count)]


def rest_pairs(count, ring):
    return [(back_place(p, count, ring), (p + 2) % count) for p in range(count)]


def order():
    return np.concatenate([np.arange(0, WIDTH, 2), np.arange(1, WIDTH, 2)])


def dft_halves():
    j, k = np.arange(HALF)[:, None], np.arange(HALF)[None, :]
    halves = []
    for odd in (0, 1):
        angle = -2.0 * np.pi * (j * (2 * k + odd) % WIDTH) / WIDTH
        re, im = np.cos(angle) / math.sqrt(WIDTH), np.sin(angle) / math.sqrt(WIDTH)
        halves.append(np.block([[re, im], [-im, re]]))
    return np.stack(halves)


def dft_tables():
    plain = dft_halves()
    full = np.concatenate([plain, plain.transpose(0, 2, 1)])
    high = full.astype(BF16)
    low = (full - high.astype(np.float64)).astype(BF16)
    return np.stack([high, low])


def transfer_phase():
    index = np.arange(WIDTH)
    freq = (((index + HALF) % WIDTH - HALF) / WIDTH)[order()]
    return (np.pi * (freq[:, None] ** 2 + freq[None, :] ** 2)).astype(np.float32)


def shuffle():
    return np.eye(WIDTH, dtype=np.float32)[order()]


def split(x):
    high = x.astype(BF16)
    return high, (x - high.astype(F32)).astype(BF16)


def dot(a, b):
    return jnp.dot(a, b, preferred_element_type=F32)


def right(t, tables, k):
    high, low = split(t)
    return dot(high, tables[0, k]) + (dot(low, tables[0, k]) + dot(high, tables[1, k]))


def left(tables, k, t):
    high, low = split(t)
    return dot(tables[0, k], high) + (dot(tables[0, k], low) + dot(tables[1, k], high))


def forward(re, im, tables):
    a = [re[:, :HALF], im[:, :HALF]]
    b = [re[:, HALF:], im[:, HALF:]]
    even = right(jnp.concatenate([a[0] + b[0], a[1] + b[1]], 1), tables, 0)
    odd = right(jnp.concatenate([a[0] - b[0], a[1] - b[1]], 1), tables, 1)
    re = jnp.concatenate([even[:, :HALF], odd[:, :HALF]], 1)
    im = jnp.concatenate([even[:, HALF:], odd[:, HALF:]], 1)
    a = [re[:HALF], im[:HALF]]
    b = [re[HALF:], im[HALF:]]
    even = left(tables, 2, jnp.concatenate([a[0] + b[0], a[1] + b[1]], 0))
    odd = left(tables, 3, jnp.concatenate([a[0] - b[0], a[1] - b[1]], 0))
    return (jnp.concatenate([even[:HALF], odd[:HALF]], 0), jnp.concatenate([even[HALF:], odd[HALF:]], 0))


def inverse(re, im, tables):
    even = left(tables, 0, jnp.concatenate([re[:HALF], im[:HALF]], 0))
    odd = left(tables, 1, jnp.concatenate([re[HALF:], im[HALF:]], 0))
    up, down = even + odd, even - odd
    re = jnp.concatenate([up[:HALF], down[:HALF]], 0)
    im = jnp.concatenate([up[HALF:], down[HALF:]], 0)
    even = right(jnp.concatenate([re[:, :HALF], im[:, :HALF]], 1), tables, 2)
    odd = right(jnp.concatenate([re[:, HALF:], im[:, HALF:]], 1), tables, 3)
    up, down = even + odd, even - odd
    return (
        jnp.concatenate([up[:, :HALF], down[:, :HALF]], 1),
        jnp.concatenate([up[:, HALF:], down[:, HALF:]], 1),
    )


def product(a_re, a_im, b_re, b_im):
    return a_re * b_re - a_im * b_im, a_re * b_im + a_im * b_re


def product_conj(a_re, a_im, b_re, b_im):
    return a_re * b_re + a_im * b_im, a_im * b_re - a_re * b_im


def constrained(u_re, u_im, amps):
    scale = amps * lax.rsqrt(u_re * u_re + u_im * u_im + 0.25)
    return u_re * scale, u_im * scale


def first_kernel(f_ref, a_ref, q_ref, tables, g_ref, *rest):
    spec_ref, grad_ref = rest[-3:-1]
    s_re, s_im = forward(f_ref[0, 0], f_ref[1, 0], tables)
    p_re, p_im = product(s_re, s_im, q_ref[0], q_ref[1])
    n_re, n_im = constrained(*inverse(p_re, p_im, tables), a_ref[0])
    n_re, n_im = forward(n_re, n_im, tables)
    spec_ref[0, 0] = n_re
    spec_ref[1, 0] = n_im
    add(g_ref, grad_ref, *product_conj(p_re - n_re, p_im - n_im, s_re, s_im))


def second_kernel(s_ref, a_ref, q_ref, tables, g_ref, *rest):
    out_ref, grad_ref = rest[-3:-1]
    s_re, s_im = s_ref[0, 0], s_ref[1, 0]
    u_re, u_im = inverse(*product(s_re, s_im, q_ref[0], q_ref[1]), tables)
    n_re, n_im = constrained(u_re, u_im, a_ref[0])
    out_ref[0, 0] = n_re
    out_ref[1, 0] = n_im
    w_re, w_im = forward(u_re - n_re, u_im - n_im, tables)
    add(g_ref, grad_ref, *product_conj(w_re, w_im, s_re, s_im))


def last_kernel(s_ref, a_ref, q_ref, tables, g_ref, other_ref, *rest):
    first_one = pl.program_id(0) == 0

    class Chosen:
        def __getitem__(self, at):
            return jnp.where(first_one, s_ref[at], other_ref[at])

    second_kernel(Chosen(), a_ref, q_ref, tables, g_ref, *rest)


def add(g_ref, grad_ref, g_re, g_im):
    @pl.when(pl.program_id(0) == 0)
    def _():
        grad_ref[...] = g_ref[...]

    grad_ref[0] += g_re
    grad_ref[1] += g_im


def tile_spec(shape, at, stride=1):
    if len(shape) == 4:
        return pl.BlockSpec((2, 1, WIDTH, WIDTH), lambda i: (0, at + i * stride, 0, 0))
    return pl.BlockSpec((1, WIDTH, WIDTH), lambda i: (at + i * stride, 0, 0))


def whole(shape):
    return pl.BlockSpec(shape, lambda i: (0,) * len(shape))


ANY = pl.BlockSpec(memory_space=pl.ANY)
PAIR = (2, WIDTH, WIDTH)


def step_call(kernel, x, x_at, amps, a_at, q, tables, grad, token, tiles, out, out_at, out_tiles, after, weight, name):
    shape = (2, out_tiles, WIDTH, WIDTH)
    more = [token, *([] if out is None else [out]), *after]
    aliases = {4: 1, 5: 2} if out is None else {4: 1, 5: 2, 6: 0}
    return pl.pallas_call(
        kernel,
        grid=(tiles,),
        in_specs=[tile_spec(x.shape, x_at), tile_spec(amps.shape, a_at), whole(PAIR), whole(tables.shape), whole(PAIR)]
        + [ANY for _ in more],
        out_specs=[tile_spec(shape, out_at), whole(PAIR), ANY],
        out_shape=[
            jax.ShapeDtypeStruct(shape, F32),
            jax.ShapeDtypeStruct(PAIR, F32),
            jax.ShapeDtypeStruct(token.shape, F32),
        ],
        input_output_aliases=aliases,
        compiler_params=pltpu.CompilerParams(vmem_limit_bytes=40 * 1024 * 1024),
        cost_estimate=pl.CostEstimate(flops=int(weight * 1_000_000_000), bytes_accessed=tiles * 400_000, transcendentals=0),
        name=name,
    )(x, amps, q, tables, grad, *more)


def last_step(x, other, amps, at, other_at, q, tables, grad, token, out):
    stride = other_at - at
    return pl.pallas_call(
        last_kernel,
        grid=(2,),
        in_specs=[whole(x.shape), tile_spec(amps.shape, at, stride), whole(PAIR), whole(tables.shape), whole(PAIR)]
        + [whole(other.shape), ANY, ANY],
        out_specs=[tile_spec(out.shape, at, stride), whole(PAIR), ANY],
        out_shape=[jax.ShapeDtypeStruct(y.shape, F32) for y in (out, grad, token)],
        input_output_aliases={4: 1, 6: 2, 7: 0},
        compiler_params=pltpu.CompilerParams(vmem_limit_bytes=40 * 1024 * 1024),
        cost_estimate=pl.CostEstimate(flops=1_000_000_000, bytes_accessed=800_000, transcendentals=0),
        name="second_step",
    )(x, amps, q, tables, grad, other, token, out)


def finish_kernel(a_ref, b_ref, ta_re, ta_im, tb_re, tb_im, mix, factor_ref, out_ref):
    a = product_conj(a_ref[0], a_ref[1], ta_re[...], ta_im[...])
    b = product_conj(b_ref[0], b_ref[1], tb_re[...], tb_im[...])
    for part in (0, 1):
        x = (a[part] + b[part]) * factor_ref[0]
        x = sum(dot(mix[1], piece) for piece in pieces(x))
        x = sum(dot(piece, mix[0]) for piece in pieces(x))
        out_ref[part, 0] = x[:, :HALF]
        out_ref[part, 1] = x[:, HALF:]


def pieces(x):
    high = x.astype(BF16)
    x = x - high.astype(F32)
    middle = x.astype(BF16)
    return high, middle, (x - middle.astype(F32)).astype(BF16)


def finished(grad_a, grad_b, turn_a, turn_b, mix, factor):
    vmem = pl.BlockSpec(memory_space=pltpu.VMEM)
    both = jnp.asarray(np.stack([mix, mix.T]).astype(BF16))
    return pl.pallas_call(
        finish_kernel,
        in_specs=[vmem] * 7 + [pl.BlockSpec(memory_space=pltpu.SMEM)],
        out_specs=vmem,
        out_shape=jax.ShapeDtypeStruct((2, 2, WIDTH, HALF), F32),
        compiler_params=pltpu.CompilerParams(vmem_limit_bytes=40 * 1024 * 1024),
        name="finish",
    )(grad_a, grad_b, *turn_a, *turn_b, both, jnp.full((1,), factor, F32))


def summed(parts):
    members = lax.axis_size("tile") * lax.axis_size("plane")
    mine = parts.reshape(members, -1, HALF)
    mine = lax.all_to_all(mine, AXES, 0, 0, tiled=True).sum(0)
    mine = jnp.broadcast_to(mine[None], (members, *mine.shape))
    total = lax.all_to_all(mine, AXES, 0, 0, tiled=True).reshape(2, 2, WIDTH, HALF)
    return total.transpose(0, 2, 1, 3).reshape(2, WIDTH, WIDTH)


def turned(distance):
    angle = distance * jnp.asarray(transfer_phase())
    return jnp.cos(angle), jnp.sin(angle)


def body(ring, fields, amplitudes, pupil, distances):
    planes, tiles_all = lax.axis_size("plane"), lax.axis_size("tile")
    fields, amps = fields[:, 0], amplitudes[0]
    count = amps.shape[0]
    factor = 1.0 / math.sqrt(STEPS * planes * tiles_all * count)
    tables = jnp.asarray(dft_tables())
    mix = shuffle()

    def sent(value, pairs):
        return lax.ppermute(value, "plane", pairs)

    ahead, behind = plane_pairs(1, planes), plane_pairs(-1, planes)
    back, rest = back_pairs(planes, ring), rest_pairs(planes, ring)

    amps_45 = sent(amps[4:6], behind)
    fields_01 = sent(fields[:, 0:2], ahead)
    distance_before = sent(distances, ahead)
    shuffled = jnp.einsum("ij,cjk,lk->cil", mix, pupil, mix, precision=lax.Precision.HIGHEST)
    turn_before, turn_here = turned(distance_before[0]), turned(distances[0])
    q_before = jnp.stack(product(shuffled[0], shuffled[1], *turn_before))
    q_here = jnp.stack(product(shuffled[0], shuffled[1], *turn_here))
    later_amps, later_fields, q_before = lax.optimization_barrier((amps, fields, q_before))
    amps_67 = sent(later_amps[6:8], behind)
    fields_23 = sent(later_fields[:, 2:4], ahead)

    grads = {"before": jnp.zeros(PAIR, F32), "here": jnp.zeros(PAIR, F32)}
    filters = {"before": q_before, "here": q_here}
    token = jnp.zeros((8, 128), F32)

    def first(which, x, x_at, a, a_at, tiles, weight, after=()):
        nonlocal token
        result, grads[which], token = step_call(
            first_kernel, x, x_at, a, a_at, filters[which], tables, grads[which], token, tiles, None, 0, tiles, after, weight, "first_step")
        return result

    out = None

    def second(x, at, tiles, weight):
        nonlocal token, out
        out, grads["before"], token = step_call(
            second_kernel, x, 0, amps, at, filters["before"], tables, grads["before"], token, tiles, out, at, count, (), weight, "second_step")

    weights = [5, 20, 0.1, 20, 3, 0.1, 1, 20]
    s_45 = sent(first("here", fields, 4, amps_45, 0, 2, weights[0]), back)
    s_6 = sent(first("here", fields, 6, amps_67, 0, 1, weights[1]), back)
    s_01 = sent(first("before", fields_01, 0, amps, 0, 2, weights[2]), ahead)
    s_7 = sent(first("here", fields, 7, amps_67, 1, 1, weights[3]), plane_pairs(2, planes))
    s_2 = sent(first("before", fields_23, 0, amps, 2, 1, weights[4]), ahead)
    s_3 = sent(first("before", fields_23, 1, amps, 3, 1, weights[5]), ahead)
    s_45 = sent(s_45, rest)
    s_6 = sent(s_6, rest)
    second(s_01, 0, 2, weights[6])
    second(s_7, 7, 1, weights[6])
    second(s_45, 4, 2, weights[6])
    second(s_2, 2, 1, weights[7])
    out, grads["before"], token = last_step(
        s_6, s_3, amps, 6, 3, filters["before"], tables, grads["before"], token, out)

    parts = finished(grads["before"], grads["here"], turn_before, turn_here, mix, 2.0 * factor)
    return (out[:, None], summed(parts))


def solution(mesh):
    placed = (P(None, "plane", "tile", None, None), P("plane", "tile", None, None), P(), P("plane"))
    ring = mesh.shape["plane"] // 2

    def step(*args):
        return body(ring, *args)

    return jax.shard_map(
        step,
        mesh=mesh,
        in_specs=placed,
        out_specs=(P(None, "plane", "tile", None, None), P()),
        check_vma=False,
    )
```
